32 devices in a mesh: groups: 2 (over y), seq: 16 (over z, x, core).
Axes of the slice: x: 2, y: 2, z: 4, core: 2. Of those that a mesh axis runs over, the one named last changes fastest.
Arguments:
- inputs: float32 [2048, 128], P(('groups', 'seq')), parts along dimension 0, may hold values from -6 to 6
- guesses: float32 [2048, 128], P(('groups', 'seq')), parts along dimension 0, may hold values from -3 to 3
- initial: float32 [256], P('groups'), parts along dimension 0, may hold values from -4 to 4
- w_input: float32 [128, 384], replicated, may hold values from -0.5 to 0.5
- w_hidden: float32 [128, 384], replicated, may hold values from -0.5 to 0.5
- biases: float32 [384], replicated, as said below
Outputs:
- trajectory: float32 [2048, 128], P(('groups', 'seq')), parts along dimension 0
The draws below stay inside these ranges and needn't reach their ends.
There are 2 independent parts, one for each index of `groups`. The reference program is written for one: setup_inputs(seed, part) draws one part's arguments, and reference() takes and returns one part's arrays. A program takes and returns all parts, laid end to end along the dimension named above; an argument that names none is the same for every part. Nothing has to cross between parts.
Inputs may be any that keep to these rules, and one draw needn't show every extreme that they name: Entries 0 to 127 are the update gate's biases, the others those of the reset gate and the candidate.
All inputs are finite; a program needn't handle non-finite values.
Results may differ from the reference program's by a relative error of at most 0.0004.
Values sent between devices are 32-bit elements; how exact they have to be, the bound alone decides.
A program may use at most 128 MiB of HBM per device.

```python
import math
import jax
import jax.numpy as jnp
from jax import lax

H = 128
DIN = 128
TOTAL = 1024


def draw_biases(key, part):
    key_rate = jax.random.fold_in(key, 11)
    key_other = jax.random.fold_in(key, 23)
    key_class = jax.random.fold_in(key, 37)
    kind = jax.random.randint(key_class, (H,), 0, 4)
    fast_lo = math.log(1.0 / 40.0)
    fast_hi = math.log(0.5)
    mid_lo = math.log(1.0 / 2000.0)
    mid_hi = math.log(1.0 / 200.0)
    slow_lo = math.log(0.5 / TOTAL)
    slow_hi = math.log(2.0 / TOTAL)
    lower = jnp.where(kind == 0, fast_lo, jnp.where(kind == 3, slow_lo, mid_lo))
    upper = jnp.where(kind == 0, fast_hi, jnp.where(kind == 3, slow_hi, mid_hi))
    others = jnp.clip(0.7 * jax.random.normal(key_other, (2 * H,), jnp.float32), -3.0, 3.0)
    fraction = jax.random.uniform(key_rate, (H,), jnp.float32, 0.0, 1.0)
    leak = jnp.exp(lower + fraction * (upper - lower))
    gate_bias = jnp.log((1.0 - leak) / leak)
    return jnp.concatenate([gate_bias, others]).astype(jnp.float32)


def block_scale(key, shape, shards, smallest, largest):
    loudness = 1.0
    for dim, blocks in shards:
        draws = jax.random.uniform(jax.random.fold_in(jax.random.fold_in(key, 6), dim), (blocks,), jnp.float32, smallest / len(shards), largest / len(shards))
        loudness = loudness * jnp.repeat(jnp.exp(draws), shape[dim] // blocks).reshape((-1,) + (1,) * (len(shape) - 1 - dim))
    return loudness


def gaussian(own_key, dims, scale, limit, split=(), dtype=jnp.bfloat16):
    factor_of = block_scale(own_key, dims, split, -0.22, 0.18) if split else 1.0
    entries = jax.random.normal(own_key, dims, jnp.float32) * scale * factor_of
    return jnp.minimum(jnp.maximum(entries, -limit), limit).astype(dtype)


def setup_inputs(seed: int = 0, part: int = 0) -> dict:
    key_list = jax.random.split(jax.random.key(seed), 7)
    part_keys = jax.random.split(jax.random.fold_in(key_list[6], part), 7)
    inputs = gaussian(part_keys[0], (TOTAL, DIN), 1.0, 6.0, ((0, 16),), jnp.float32)
    guesses = gaussian(part_keys[1], (TOTAL, H), 0.5, 3.0, ((0, 16),), jnp.float32)
    initial = gaussian(part_keys[2], (H,), 1.0, 4.0, (), jnp.float32)
    w_input = gaussian(key_list[3], (DIN, 3 * H), DIN ** -0.5, 0.5, (), jnp.float32)
    w_hidden = gaussian(key_list[4], (H, 3 * H), H ** -0.5, 0.5, (), jnp.float32)
    biases = draw_biases(jax.random.fold_in(key_list[6], 71), part)
    return dict(inputs=inputs, guesses=guesses, initial=initial, w_input=w_input, w_hidden=w_hidden, biases=biases)


def coefficients(previous, pre, rec, width):
    pz, pr, pn = pre[:, :width], pre[:, width:2 * width], pre[:, 2 * width:]
    cz, cr, cn = rec[:, :width], rec[:, width:2 * width], rec[:, 2 * width:]
    update = jax.nn.sigmoid(pz + cz)
    reset = jax.nn.sigmoid(pr + cr)
    cand = jnp.tanh(pn + reset * cn)
    value = (1.0 - update) * cand + update * previous
    coef_update = (previous - cand) * update * (1.0 - update)
    coef_cand = (1.0 - update) * (1.0 - cand * cand) * reset
    coef_reset = (1.0 - update) * (1.0 - cand * cand) * cn * reset * (1.0 - reset)
    offset = value - (update * previous + coef_update * cz + coef_cand * cn + coef_reset * cr)
    return update, coef_update, coef_cand, coef_reset, offset


def reference(inputs, guesses, initial, w_input, w_hidden, biases):
    width = guesses.shape[1]
    previous = jnp.concatenate([initial[None, :], guesses[:-1]], axis=0)
    pre = jnp.dot(inputs, w_input, precision=lax.Precision.HIGHEST, preferred_element_type=jnp.float32) + biases
    rec = jnp.dot(previous, w_hidden, precision=lax.Precision.HIGHEST, preferred_element_type=jnp.float32)
    update, coef_update, coef_cand, coef_reset, offset = coefficients(previous, pre, rec, width)

    def advance(state, row_items):
        upd, cu, cc, cr_, off = row_items
        prod = jnp.dot(state, w_hidden, precision=lax.Precision.HIGHEST, preferred_element_type=jnp.float32)
        new_state = upd * state + cu * prod[:width] + cc * prod[2 * width:] + cr_ * prod[width:2 * width] + off
        return new_state, new_state

    final_state, trajectory = lax.scan(advance, initial, (update, coef_update, coef_cand, coef_reset, offset))
    return trajectory
```

```python
import functools
import math

import jax
import jax.numpy as jnp
from jax import lax
from jax.experimental import pallas as pl
from jax.experimental.pallas import tpu as pltpu
from jax.sharding import PartitionSpec as P

TAIL = 16
SENT = 8
BATCH = 4


def split(value):
    high = value.astype(jnp.bfloat16)
    low = (value - high.astype(jnp.float32)).astype(jnp.bfloat16)
    return high, low


def product(left, right):
    lh, ll = split(left)
    rh, rl = split(right)
    parts = jnp.concatenate([rh, rl], axis=1)
    both = jnp.dot(
        jnp.concatenate([lh, ll], axis=1),
        jnp.concatenate([parts, parts], axis=0),
        preferred_element_type=jnp.float32,
    )
    width = right.shape[1]
    return both[:, :width] + both[:, width:]


def compose(early, late):
    width = late.shape[1]
    moved = product(early, late[:width])
    return moved[:width], moved[width:] + late[width:]


def column(row):
    width = row.shape[1]
    return jnp.broadcast_to(row, (width, width)).T


def kernel(
    count, group,
    inputs, guesses, initial, w_input, w_hidden, biases, out,
    maps, prev, upd, cz_, cn_, cr_, off, arrived, incl, excl, state, state_next,
    row_send, row_recv, map_send, map_recv, state_send, state_recv,
):
    steps, width = guesses.shape
    levels = int(math.log2(group))
    me = lax.axis_index("seq")
    place = lax.rem(me, group)
    first_group = me < group
    last_group = me >= count - group
    leader = place == group - 1
    forwards = jnp.logical_and(leader, jnp.logical_not(last_group))

    def upper(level):
        return lax.rem(lax.div(me, 2**level), 2) == 1

    def sends(level):
        return lax.rem(me, 2 ** (level + 1)) == 2**level - 1

    def row_copy():
        return pltpu.make_async_remote_copy(
            src_ref=guesses.at[pl.ds(steps - 8, 8)], dst_ref=prev.at[pl.ds(0, 8)],
            send_sem=row_send, recv_sem=row_recv, device_id={"seq": me + 1})

    def map_copy(level, which):
        src = maps.at[steps - 1] if level == 0 else incl.at[level - 1]
        return pltpu.make_async_remote_copy(
            src_ref=src.at[pl.ds(0, width + SENT)],
            dst_ref=arrived.at[level, pl.ds(0, width + SENT)],
            send_sem=map_send.at[2**level - 1 + which], recv_sem=map_recv.at[level],
            device_id={"seq": me + 1 + which})

    def state_copy(which):
        return pltpu.make_async_remote_copy(
            src_ref=state_next, dst_ref=state,
            send_sem=state_send.at[which], recv_sem=state_recv,
            device_id={"seq": me + 1 + which})

    barrier = pltpu.get_barrier_semaphore()

    @pl.when(me > 0)
    def _():
        pl.semaphore_signal(barrier, 1, device_id={"seq": me - 1})

    for level in range(levels):
        @pl.when(upper(level))
        def _():
            source = lax.div(me, 2**level) * 2**level - 1
            pl.semaphore_signal(barrier, 1, device_id={"seq": source})

    @pl.when(jnp.logical_not(first_group))
    def _():
        pl.semaphore_signal(barrier, 1, device_id={"seq": lax.div(me, group) * group - 1})

    copies = 1 + group * forwards.astype(jnp.int32)
    for level in range(levels):
        copies += 2**level * sends(level).astype(jnp.int32)

    @pl.when(me < count - 1)
    def _():
        pl.semaphore_wait(barrier, copies)

    @pl.when(me < count - 1)
    def _():
        row_copy().start()

    prev[pl.ds(8, steps), :] = guesses[...]

    @pl.when(me == 0)
    def _():
        prev[pl.ds(7, 1), :] = initial[...][None, :]

    pre = product(inputs[...], w_input[...]) + biases[...][None, :]

    @pl.when(me > 0)
    def _():
        row_copy().wait_recv()

    previous = prev[pl.ds(7, steps), :]
    rec = product(previous, w_hidden[...])
    pz, pr, pn = (pre[:, :width], pre[:, width : 2 * width], pre[:, 2 * width :])
    cz, cr, cn = (rec[:, :width], rec[:, width : 2 * width], rec[:, 2 * width :])
    update = jax.nn.sigmoid(pz + cz)
    reset = jax.nn.sigmoid(pr + cr)
    cand = jnp.tanh(pn + reset * cn)
    value = (1.0 - update) * cand + update * previous
    coef_update = (previous - cand) * update * (1.0 - update)
    coef_cand = (1.0 - update) * (1.0 - cand * cand) * reset
    coef_reset = (1.0 - update) * (1.0 - cand * cand) * cn * reset * (1.0 - reset)
    upd[...] = update
    cz_[...] = coef_update
    cn_[...] = coef_cand
    cr_[...] = coef_reset
    off[...] = value - (update * previous + coef_update * cz + coef_cand * cn + coef_reset * cr)

    rows = lax.broadcasted_iota(jnp.int32, (width, width), 0)
    cols = lax.broadcasted_iota(jnp.int32, (width, width), 1)
    top = lax.broadcasted_iota(jnp.int32, (TAIL, width), 0) == 0

    def step_map(t, _):
        one = pl.ds(t, 1)
        maps[t, :width, :] = (
            jnp.where(rows == cols, upd[one, :], 0.0)
            + cz_[one, :] * w_hidden[:, :width]
            + cr_[one, :] * w_hidden[:, width : 2 * width]
            + cn_[one, :] * w_hidden[:, 2 * width :]
        )
        maps[t, width:, :] = jnp.where(top, off[one, :], 0.0)
        return 0

    lax.fori_loop(0, steps, step_map, 0)

    def sweep(first, stride, distance, number):
        batch = min(BATCH, number)

        def some(start, size):
            where = [start + stride * j for j in range(size)]
            news = [compose(maps[i - distance], maps[i]) for i in where]
            for i, (new_map, new_tail) in zip(where, news):
                maps[i, :width, :] = new_map
                maps[i, width:, :] = new_tail

        def body(j, _):
            some(first + j * (stride * batch), batch)
            return 0

        whole = number // batch
        if whole > 1:
            lax.fori_loop(0, whole, body, 0)
        else:
            some(first, batch)
        if number % batch:
            some(first + whole * batch * stride, number % batch)

    distance = 1
    while distance < steps:
        sweep(2 * distance - 1, 2 * distance, distance, steps // (2 * distance))
        distance *= 2

    down = []
    distance = steps // 4
    while distance >= 1:
        down.append((3 * distance - 1, 2 * distance, distance, steps // (2 * distance) - 1))
        distance //= 2

    eye = jnp.where(rows == cols, 1.0, 0.0)
    excl[:width, :] = eye
    excl[width:, :] = jnp.zeros((TAIL, width), jnp.float32)
    share = {0: down[:-2], 1: down[-2:-1]}
    for level in range(levels):
        @pl.when(sends(level))
        def _():
            for which in range(2**level):
                map_copy(level, 2**level - 1 - which).start()

        for item in share.get(level, ()):
            sweep(*item)

        held = maps.at[steps - 1] if level == 0 else incl.at[level - 1]

        @pl.when(upper(level))
        def _():
            map_copy(level, 0).wait_recv()
            arrived[level, pl.ds(width + SENT, TAIL - SENT), :] = jnp.zeros(
                (TAIL - SENT, width), jnp.float32)
            early = arrived[level]
            new_map, new_tail = compose(early, held[...])
            incl[level, :width, :] = new_map
            incl[level, width:, :] = new_tail
            new_map, new_tail = compose(early, excl[...])
            excl[:width, :] = new_map
            excl[width:, :] = new_tail

        @pl.when(jnp.logical_not(upper(level)))
        def _():
            incl[level] = held[...]

    @pl.when(first_group)
    def _():
        state[...] = jnp.broadcast_to(initial[...][None, :], state.shape)

    @pl.when(forwards)
    def _():
        @pl.when(jnp.logical_not(first_group))
        def _():
            state_copy(0).wait_recv()
        whole = incl.at[levels - 1]
        moved = jnp.sum(column(state[0:1, :]) * whole[:width, :], axis=0, keepdims=True)
        state_next[...] = jnp.broadcast_to(moved + whole[width : width + 1, :], state_next.shape)
        for which in range(group):
            state_copy(group - 1 - which).start()

    for item in down[-1:]:
        sweep(*item)

    @pl.when(jnp.logical_not(jnp.logical_or(forwards, first_group)))
    def _():
        state_copy(0).wait_recv()

    entry = jnp.sum(column(state[0:1, :]) * excl[:width, :], axis=0, keepdims=True)
    across = column(entry + excl[width : width + 1, :])

    def finish(j, _):
        lines = []
        for k in range(8):
            t = j * 8 + k
            line = jnp.sum(across * maps[t, :width, :], axis=0, keepdims=True)
            lines.append(line + maps[t, width : width + 1, :])
        out[pl.ds(pl.multiple_of(j * 8, 8), 8), :] = jnp.concatenate(lines, axis=0)
        return 0

    lax.fori_loop(0, steps // 8, finish, 0)

    @pl.when(me < count - 1)
    def _():
        row_copy().wait_send()

    for level in range(levels):
        @pl.when(sends(level))
        def _():
            for which in range(2**level):
                map_copy(level, which).wait_send()

    @pl.when(forwards)
    def _():
        for which in range(group):
            state_copy(which).wait_send()


def solution(mesh):
    count = mesh.shape["seq"]
    group = 4

    def per_device(inputs, guesses, initial, w_input, w_hidden, biases):
        steps, width = guesses.shape
        levels = int(math.log2(group))
        full = width + TAIL
        line = pltpu.VMEM((steps, width), jnp.float32)
        return pl.pallas_call(
            functools.partial(kernel, count, group),
            out_shape=jax.ShapeDtypeStruct((steps, width), jnp.float32),
            in_specs=[pl.BlockSpec(memory_space=pltpu.VMEM)] * 6,
            out_specs=pl.BlockSpec(memory_space=pltpu.VMEM),
            scratch_shapes=[
                pltpu.VMEM((steps, full, width), jnp.float32),
                pltpu.VMEM((steps + 8, width), jnp.float32),
                line, line, line, line, line,
                pltpu.VMEM((levels, full, width), jnp.float32),
                pltpu.VMEM((levels, full, width), jnp.float32),
                pltpu.VMEM((full, width), jnp.float32),
                pltpu.VMEM((8, width), jnp.float32),
                pltpu.VMEM((8, width), jnp.float32),
                pltpu.SemaphoreType.DMA,
                pltpu.SemaphoreType.DMA,
                pltpu.SemaphoreType.DMA((group - 1,)),
                pltpu.SemaphoreType.DMA((levels,)),
                pltpu.SemaphoreType.DMA((group,)),
                pltpu.SemaphoreType.DMA,
            ],
            compiler_params=pltpu.CompilerParams(
                collective_id=0, has_side_effects=True, vmem_limit_bytes=32 * 2**20),
        )(inputs, guesses, initial, w_input, w_hidden, biases)

    placed = (P(("groups", "seq"), None), P(("groups", "seq"), None), P("groups"), P(), P(), P())
    return jax.shard_map(
        per_device,
        mesh=mesh,
        in_specs=placed,
        out_specs=P(("groups", "seq"), None),
        check_vma=False,
    )
```

```python
import functools
import math

import jax
import jax.numpy as jnp
from jax import lax
from jax.experimental import pallas as pl
from jax.experimental.pallas import tpu as pltpu
from jax.sharding import PartitionSpec as P

TAIL = 16
SENT = 8
BATCH = 4
PAIRS = 3


def split(value):
    high = value.astype(jnp.bfloat16)
    low = (value - high.astype(jnp.float32)).astype(jnp.bfloat16)
    return high, low


def product(left, right):
    lh, ll = split(left)
    rh, rl = split(right)
    parts = jnp.concatenate([rh, rl], axis=1)
    both = jnp.dot(
        jnp.concatenate([lh, ll], axis=1),
        jnp.concatenate([parts, parts], axis=0),
        preferred_element_type=jnp.float32,
    )
    width = right.shape[1]
    return both[:, :width] + both[:, width:]


def compose(early, late):
    width = late.shape[1]
    moved = product(early, late[:width])
    return moved[:width], moved[width:] + late[width:]


def column(row):
    width = row.shape[1]
    return jnp.broadcast_to(row, (width, width)).T


def gates(previous, pre, rec):
    width = previous.shape[1]
    pz, pr, pn = (pre[:, :width], pre[:, width : 2 * width], pre[:, 2 * width :])
    cz, cr, cn = (rec[:, :width], rec[:, width : 2 * width], rec[:, 2 * width :])
    update = jax.nn.sigmoid(pz + cz)
    reset = jax.nn.sigmoid(pr + cr)
    cand = jnp.tanh(pn + reset * cn)
    value = (1.0 - update) * cand + update * previous
    coef_update = (previous - cand) * update * (1.0 - update)
    coef_cand = (1.0 - update) * (1.0 - cand * cand) * reset
    coef_reset = (1.0 - update) * (1.0 - cand * cand) * cn * reset * (1.0 - reset)
    offset = value - (update * previous + coef_update * cz + coef_cand * cn + coef_reset * cr)
    return update, coef_update, coef_reset, coef_cand, offset


def kernel(
    count, group,
    inputs_hbm, guesses_hbm, initial_hbm, w_input_hbm, w_hidden_hbm, biases_hbm, out,
    inputs, initial, w_input, w_hidden, biases, packed,
    maps, prev, landed, pre_first, coefs, odd, arrived, incl, excl, state, state_next,
    load_sem, row_send, row_recv, map_send, map_recv, state_send, state_recv,
):
    steps, width = inputs.shape
    levels = int(math.log2(group))
    me = lax.axis_index("seq")
    place = lax.rem(me, group)
    first_group = me < group
    last_group = me >= count - group
    leader = place == group - 1
    forwards = jnp.logical_and(leader, jnp.logical_not(last_group))

    def upper(level):
        return lax.rem(lax.div(me, 2**level), 2) == 1

    def sends(level):
        return lax.rem(me, 2 ** (level + 1)) == 2**level - 1

    def row_copy():
        return pltpu.make_async_remote_copy(
            src_ref=prev.at[pl.ds(steps, 8)], dst_ref=landed,
            send_sem=row_send, recv_sem=row_recv, device_id={"seq": me + 1})

    def map_copy(level, which):
        src = maps.at[steps // 2 - 1] if level == 0 else incl.at[level - 1]
        return pltpu.make_async_remote_copy(
            src_ref=src.at[pl.ds(0, width + SENT)],
            dst_ref=arrived.at[level, pl.ds(0, width + SENT)],
            send_sem=map_send.at[2**level - 1 + which], recv_sem=map_recv.at[level],
            device_id={"seq": me + 1 + which})

    def state_copy(which):
        return pltpu.make_async_remote_copy(
            src_ref=state_next, dst_ref=state,
            send_sem=state_send.at[which], recv_sem=state_recv,
            device_id={"seq": me + 1 + which})

    loads = [
        pltpu.make_async_copy(src, dst, load_sem.at[k])
        for k, (src, dst) in enumerate([
            (w_hidden_hbm, w_hidden), (w_input_hbm, w_input),
            (guesses_hbm, prev.at[pl.ds(8, steps)]), (inputs_hbm, inputs),
            (initial_hbm, initial), (biases_hbm, biases)])
    ]
    for load in loads:
        load.start()

    barrier = pltpu.get_barrier_semaphore()

    @pl.when(me > 0)
    def _():
        pl.semaphore_signal(barrier, 1, device_id={"seq": me - 1})

    for level in range(levels):
        @pl.when(upper(level))
        def _():
            source = lax.div(me, 2**level) * 2**level - 1
            pl.semaphore_signal(barrier, 1, device_id={"seq": source})

    @pl.when(jnp.logical_not(first_group))
    def _():
        pl.semaphore_signal(barrier, 1, device_id={"seq": lax.div(me, group) * group - 1})

    for load in loads:
        load.wait()

    prev[pl.ds(0, 8), :] = jnp.broadcast_to(initial[...][None, :], (8, width))
    high, low = split(w_hidden[...])
    for half in range(2):
        packed[half * width : (half + 1) * width, : 3 * width] = high
        packed[half * width : (half + 1) * width, 3 * width :] = low

    def recurrent(rows):
        both = jnp.dot(
            jnp.concatenate(split(rows), axis=1), packed[...],
            preferred_element_type=jnp.float32)
        return both[:, : 3 * width] + both[:, 3 * width :]

    pre = product(inputs[...], w_input[...]) + biases[...][None, :]
    pre_first[...] = pre[:16]
    previous = prev[pl.ds(7, steps), :]
    for k, part in enumerate(gates(previous, pre, recurrent(previous))):
        coefs[k] = part

    copies = 1 + group * forwards.astype(jnp.int32)
    for level in range(levels):
        copies += 2**level * sends(level).astype(jnp.int32)

    @pl.when(me < count - 1)
    def _():
        pl.semaphore_wait(barrier, copies)
        row_copy().start()

    rows = lax.broadcasted_iota(jnp.int32, (width, width), 0)
    cols = lax.broadcasted_iota(jnp.int32, (width, width), 1)
    top = lax.broadcasted_iota(jnp.int32, (TAIL, width), 0) == 0

    def step_map(t):
        one = pl.ds(t, 1)
        upd, cz, cr, cn, off = [coefs[k, one, :] for k in range(5)]
        body = (
            jnp.where(rows == cols, upd, 0.0)
            + cz * w_hidden[:, :width]
            + cr * w_hidden[:, width : 2 * width]
            + cn * w_hidden[:, 2 * width :]
        )
        return jnp.concatenate([body, jnp.where(top, off, 0.0)], axis=0)

    def store(ref, new):
        ref[:width, :] = new[0]
        ref[width:, :] = new[1]

    def pair(i):
        store(maps.at[i], compose(step_map(2 * i), step_map(2 * i + 1)))

    def pairs(start, size):
        news = [compose(step_map(2 * i), step_map(2 * i + 1))
                for i in [start + k for k in range(size)]]
        for k, new in enumerate(news):
            store(maps.at[start + k], new)

    def pairs_body(j, _):
        pairs(1 + PAIRS * j, PAIRS)
        return 0

    number = steps // 2
    whole = (number - 1) // PAIRS
    lax.fori_loop(0, whole, pairs_body, 0)

    @pl.when(me > 0)
    def _():
        row_copy().wait_recv()
        prev[pl.ds(7, 1), :] = landed[pl.ds(7, 1), :]
        fixed = prev[pl.ds(7, 16), :]
        for k, part in enumerate(gates(fixed, pre_first[...], recurrent(fixed))):
            coefs[k, :16, :] = part

    for i in [0] + list(range(1 + PAIRS * whole, number)):
        pair(i)

    def sweep(first, stride, distance, number):
        batch = min(BATCH, number)

        def some(start, size):
            where = [start + stride * j for j in range(size)]
            news = [compose(maps[i - distance], maps[i]) for i in where]
            for i, new in zip(where, news):
                store(maps.at[i], new)

        def body(j, _):
            some(first + j * (stride * batch), batch)
            return 0

        whole = number // batch
        if whole > 1:
            lax.fori_loop(0, whole, body, 0)
        else:
            some(first, batch)
        if number % batch:
            some(first + whole * batch * stride, number % batch)

    distance = 1
    while distance < number:
        sweep(2 * distance - 1, 2 * distance, distance, number // (2 * distance))
        distance *= 2

    down = []
    distance = number // 4
    while distance >= 1:
        down.append((3 * distance - 1, 2 * distance, distance, number // (2 * distance) - 1))
        distance //= 2

    excl[:width, :] = jnp.where(rows == cols, 1.0, 0.0)
    excl[width:, :] = jnp.zeros((TAIL, width), jnp.float32)
    share = {0: down[:-1]}
    for level in range(levels):
        @pl.when(sends(level))
        def _():
            for which in range(2**level):
                map_copy(level, 2**level - 1 - which).start()

        for item in share.get(level, ()):
            sweep(*item)

        held = maps.at[number - 1] if level == 0 else incl.at[level - 1]

        @pl.when(upper(level))
        def _():
            map_copy(level, 0).wait_recv()
            arrived[level, pl.ds(width + SENT, TAIL - SENT), :] = jnp.zeros(
                (TAIL - SENT, width), jnp.float32)
            early = arrived[level]
            store(incl.at[level], compose(early, held[...]))
            store(excl, compose(early, excl[...]))

        @pl.when(jnp.logical_not(upper(level)))
        def _():
            incl[level] = held[...]

    @pl.when(first_group)
    def _():
        state[...] = jnp.broadcast_to(initial[...][None, :], state.shape)

    @pl.when(forwards)
    def _():
        @pl.when(jnp.logical_not(first_group))
        def _():
            state_copy(0).wait_recv()
        whole = incl.at[levels - 1]
        moved = jnp.sum(column(state[0:1, :]) * whole[:width, :], axis=0, keepdims=True)
        state_next[...] = jnp.broadcast_to(
            moved + whole[width : width + 1, :], state_next.shape)
        for which in range(group):
            state_copy(group - 1 - which).start()

    for item in down[-1:]:
        sweep(*item)

    @pl.when(jnp.logical_not(jnp.logical_or(forwards, first_group)))
    def _():
        state_copy(0).wait_recv()

    entry = jnp.sum(column(state[0:1, :]) * excl[:width, :], axis=0, keepdims=True)
    entry = entry + excl[width : width + 1, :]
    across = column(entry)
    odd[0:8, :] = jnp.broadcast_to(entry, (8, width))

    def finish(j, _):
        lines = []
        for k in range(8):
            i = j * 8 + k
            line = jnp.sum(across * maps[i, :width, :], axis=0, keepdims=True)
            lines.append(line + maps[i, width : width + 1, :])
        odd[pl.ds(pl.multiple_of(8 + j * 8, 8), 8), :] = jnp.concatenate(lines, axis=0)
        return 0

    lax.fori_loop(0, number // 8, finish, 0)

    before = odd[pl.ds(7, number), :]
    rec = recurrent(before)
    even = pl.ds(0, number, 2)
    upd, cz, cr, cn, off = [coefs[k, even, :] for k in range(5)]
    out[even, :] = (
        upd * before + cz * rec[:, :width] + cr * rec[:, width : 2 * width]
        + cn * rec[:, 2 * width :] + off
    )
    out[pl.ds(1, number, 2), :] = odd[pl.ds(8, number), :]

    @pl.when(me < count - 1)
    def _():
        row_copy().wait_send()

    for level in range(levels):
        @pl.when(sends(level))
        def _():
            for which in range(2**level):
                map_copy(level, which).wait_send()

    @pl.when(forwards)
    def _():
        for which in range(group):
            state_copy(which).wait_send()


def solution(mesh):
    count = mesh.shape["seq"]
    group = 4

    def per_device(inputs, guesses, initial, w_input, w_hidden, biases):
        steps, width = guesses.shape
        levels = int(math.log2(group))
        full = width + TAIL
        line = pltpu.VMEM((steps, width), jnp.float32)
        return pl.pallas_call(
            functools.partial(kernel, count, group),
            out_shape=jax.ShapeDtypeStruct((steps, width), jnp.float32),
            in_specs=[pl.BlockSpec(memory_space=pl.ANY)] * 6,
            out_specs=pl.BlockSpec(memory_space=pltpu.VMEM),
            scratch_shapes=[
                pltpu.VMEM((steps, width), jnp.float32),
                pltpu.VMEM((width,), jnp.float32),
                pltpu.VMEM((width, 3 * width), jnp.float32),
                pltpu.VMEM((width, 3 * width), jnp.float32),
                pltpu.VMEM((3 * width,), jnp.float32),
                pltpu.VMEM((2 * width, 6 * width), jnp.bfloat16),
                pltpu.VMEM((steps // 2, full, width), jnp.float32),
                pltpu.VMEM((steps + 8, width), jnp.float32),
                pltpu.VMEM((8, width), jnp.float32),
                pltpu.VMEM((16, 3 * width), jnp.float32),
                pltpu.VMEM((5, steps, width), jnp.float32),
                pltpu.VMEM((steps // 2 + 8, width), jnp.float32),
                pltpu.VMEM((levels, full, width), jnp.float32),
                pltpu.VMEM((levels, full, width), jnp.float32),
                pltpu.VMEM((full, width), jnp.float32),
                pltpu.VMEM((8, width), jnp.float32),
                pltpu.VMEM((8, width), jnp.float32),
                pltpu.SemaphoreType.DMA((6,)),
                pltpu.SemaphoreType.DMA,
                pltpu.SemaphoreType.DMA,
                pltpu.SemaphoreType.DMA((group - 1,)),
                pltpu.SemaphoreType.DMA((levels,)),
                pltpu.SemaphoreType.DMA((group,)),
                pltpu.SemaphoreType.DMA,
            ],
            compiler_params=pltpu.CompilerParams(
                collective_id=0, has_side_effects=True, vmem_limit_bytes=56 * 2**20),
        )(inputs, guesses, initial, w_input, w_hidden, biases)

    placed = (P(("groups", "seq"), None), P(("groups", "seq"), None), P("groups"), P(), P(), P())
    return jax.shard_map(
        per_device,
        mesh=mesh,
        in_specs=placed,
        out_specs=P(("groups", "seq"), None),
        check_vma=False,
    )
```

```python
import functools
import math

import jax
import jax.numpy as jnp
from jax import lax
from jax.experimental import pallas as pl
from jax.experimental.pallas import tpu as pltpu
from jax.sharding import PartitionSpec as P

TAIL = 16
SENT = 8
BATCH = 4
PAIRS = 3


def split(value):
    high = value.astype(jnp.bfloat16)
    low = (value - high.astype(jnp.float32)).astype(jnp.bfloat16)
    return high, low


def product(left, right):
    lh, ll = split(left)
    rh, rl = split(right)
    parts = jnp.concatenate([rh, rl], axis=1)
    both = jnp.dot(
        jnp.concatenate([lh, ll], axis=1),
        jnp.concatenate([parts, parts], axis=0),
        preferred_element_type=jnp.float32,
    )
    width = right.shape[1]
    return both[:, :width] + both[:, width:]


def compose(early, late):
    width = late.shape[1]
    moved = product(early, late[:width])
    return moved[:width], moved[width:] + late[width:]


def column(row):
    width = row.shape[1]
    return jnp.broadcast_to(row, (width, width)).T


def gates(previous, pre, rec):
    width = previous.shape[1]
    pz, pr, pn = (pre[:, :width], pre[:, width : 2 * width], pre[:, 2 * width :])
    cz, cr, cn = (rec[:, :width], rec[:, width : 2 * width], rec[:, 2 * width :])
    update = jax.nn.sigmoid(pz + cz)
    reset = jax.nn.sigmoid(pr + cr)
    cand = jnp.tanh(pn + reset * cn)
    value = (1.0 - update) * cand + update * previous
    coef_update = (previous - cand) * update * (1.0 - update)
    coef_cand = (1.0 - update) * (1.0 - cand * cand) * reset
    coef_reset = (1.0 - update) * (1.0 - cand * cand) * cn * reset * (1.0 - reset)
    offset = value - (update * previous + coef_update * cz + coef_cand * cn + coef_reset * cr)
    return update, coef_update, coef_reset, coef_cand, offset


def store(ref, new):
    width = new[0].shape[0]
    ref[:width, :] = new[0]
    ref[width:, :] = new[1]


def exclude(level, me, excl, arrived, upper):
    came = jnp.logical_and(upper(level), me >= 2 ** (level + 1))
    below = lax.rem(me, 2**level) > 0

    @pl.when(jnp.logical_and(came, below))
    def _():
        store(excl, compose(arrived[level], excl[...]))

    @pl.when(jnp.logical_and(came, jnp.logical_not(below)))
    def _():
        excl[...] = arrived[level]


def kernel(
    count, group,
    inputs_hbm, guesses_hbm, initial_hbm, w_input_hbm, w_hidden_hbm, biases_hbm, out,
    inputs, initial, w_input, w_hidden, biases, packed,
    maps, prev, landed, pre_first, coefs, odd, arrived, incl, excl, state, state_next,
    load_sem, row_send, row_recv, map_send, map_recv, state_send, state_recv,
):
    steps, width = inputs.shape
    levels = int(math.log2(group))
    me = lax.axis_index("seq")
    place = lax.rem(me, group)
    first_group = me < group
    last_group = me >= count - group
    leader = place == group - 1
    forwards = jnp.logical_and(leader, jnp.logical_not(last_group))

    def upper(level):
        return lax.rem(lax.div(me, 2**level), 2) == 1

    def sends(level):
        return lax.rem(me, 2 ** (level + 1)) == 2**level - 1

    def row_copy():
        return pltpu.make_async_remote_copy(
            src_ref=prev.at[pl.ds(steps, 8)], dst_ref=landed,
            send_sem=row_send, recv_sem=row_recv, device_id={"seq": me + 1})

    def map_copy(level, which):
        src = maps.at[steps // 2 - 1] if level == 0 else incl.at[level - 1]
        return pltpu.make_async_remote_copy(
            src_ref=src.at[pl.ds(0, width + SENT)],
            dst_ref=arrived.at[level, pl.ds(0, width + SENT)],
            send_sem=map_send.at[2**level - 1 + which], recv_sem=map_recv.at[level],
            device_id={"seq": me + 1 + which})

    def state_copy(which):
        return pltpu.make_async_remote_copy(
            src_ref=state_next, dst_ref=state,
            send_sem=state_send.at[which], recv_sem=state_recv,
            device_id={"seq": me + 1 + which})

    loads = [
        pltpu.make_async_copy(src, dst, load_sem.at[k])
        for k, (src, dst) in enumerate([
            (w_hidden_hbm, w_hidden), (w_input_hbm, w_input),
            (guesses_hbm, prev.at[pl.ds(8, steps)]), (inputs_hbm, inputs),
            (initial_hbm, initial), (biases_hbm, biases)])
    ]
    for load in loads:
        load.start()

    barrier = pltpu.get_barrier_semaphore()

    @pl.when(me > 0)
    def _():
        pl.semaphore_signal(barrier, 1, device_id={"seq": me - 1})

    for level in range(levels):
        @pl.when(upper(level))
        def _():
            source = lax.div(me, 2**level) * 2**level - 1
            pl.semaphore_signal(barrier, 1, device_id={"seq": source})

    @pl.when(jnp.logical_not(first_group))
    def _():
        pl.semaphore_signal(barrier, 1, device_id={"seq": lax.div(me, group) * group - 1})

    for load in loads:
        load.wait()

    prev[pl.ds(0, 8), :] = jnp.broadcast_to(initial[...][None, :], (8, width))
    high, low = split(w_hidden[...])
    for half in range(2):
        packed[half * width : (half + 1) * width, : 3 * width] = high
        packed[half * width : (half + 1) * width, 3 * width :] = low

    def recurrent(rows):
        both = jnp.dot(
            jnp.concatenate(split(rows), axis=1), packed[...],
            preferred_element_type=jnp.float32)
        return both[:, : 3 * width] + both[:, 3 * width :]

    pre = product(inputs[...], w_input[...]) + biases[...][None, :]
    pre_first[...] = pre[:16]
    previous = prev[pl.ds(7, steps), :]
    for k, part in enumerate(gates(previous, pre, recurrent(previous))):
        coefs[k] = part

    copies = 1 + group * forwards.astype(jnp.int32)
    for level in range(levels):
        copies += 2**level * sends(level).astype(jnp.int32)

    @pl.when(me < count - 1)
    def _():
        pl.semaphore_wait(barrier, copies)
        row_copy().start()

    rows = lax.broadcasted_iota(jnp.int32, (width, width), 0)
    cols = lax.broadcasted_iota(jnp.int32, (width, width), 1)
    top = lax.broadcasted_iota(jnp.int32, (TAIL, width), 0) == 0

    def step_map(t):
        one = pl.ds(t, 1)
        upd, cz, cr, cn, off = [coefs[k, one, :] for k in range(5)]
        body = (
            jnp.where(rows == cols, upd, 0.0)
            + cz * w_hidden[:, :width]
            + cr * w_hidden[:, width : 2 * width]
            + cn * w_hidden[:, 2 * width :]
        )
        return jnp.concatenate([body, jnp.where(top, off, 0.0)], axis=0)

    def pair(i):
        store(maps.at[i], compose(step_map(2 * i), step_map(2 * i + 1)))

    def pairs(start, size):
        news = [compose(step_map(2 * i), step_map(2 * i + 1))
                for i in [start + k for k in range(size)]]
        for k, new in enumerate(news):
            store(maps.at[start + k], new)

    def pairs_body(j, _):
        pairs(1 + PAIRS * j, PAIRS)
        return 0

    number = steps // 2
    whole = (number - 1) // PAIRS
    lax.fori_loop(0, whole, pairs_body, 0)

    @pl.when(me > 0)
    def _():
        row_copy().wait_recv()
        prev[pl.ds(7, 1), :] = landed[pl.ds(7, 1), :]
        fixed = prev[pl.ds(7, 16), :]
        for k, part in enumerate(gates(fixed, pre_first[...], recurrent(fixed))):
            coefs[k, :16, :] = part

    for i in [0] + list(range(1 + PAIRS * whole, number)):
        pair(i)

    def sweep(first, stride, distance, number):
        batch = min(BATCH, number)

        def some(start, size):
            where = [start + stride * j for j in range(size)]
            news = [compose(maps[i - distance], maps[i]) for i in where]
            for i, new in zip(where, news):
                store(maps.at[i], new)

        def body(j, _):
            some(first + j * (stride * batch), batch)
            return 0

        whole = number // batch
        if whole > 1:
            lax.fori_loop(0, whole, body, 0)
        else:
            some(first, batch)
        if number % batch:
            some(first + whole * batch * stride, number % batch)

    distance = 1
    while distance < number:
        sweep(2 * distance - 1, 2 * distance, distance, number // (2 * distance))
        distance *= 2

    down = []
    distance = number // 4
    while distance >= 1:
        down.append((3 * distance - 1, 2 * distance, distance, number // (2 * distance) - 1))
        distance //= 2

    def held(level):
        return maps.at[number - 1] if level == 0 else incl.at[level - 1]

    def forward(ref, targets):
        moved = jnp.sum(column(state[0:1, :]) * ref[:width, :], axis=0, keepdims=True)
        state_next[...] = jnp.broadcast_to(
            moved + ref[width : width + 1, :], state_next.shape)
        for which in range(targets):
            state_copy(targets - 1 - which).start()

    def wait_state():
        state_copy(0).wait_recv()

    share = {0: down[:-2], 1: down[-2:-1]}

    @pl.when(me == 0)
    def _():
        state[...] = jnp.broadcast_to(initial[...][None, :], state.shape)
        forward(held(0), 1)

    excl[:width, :] = jnp.where(rows == cols, 1.0, 0.0)
    excl[width:, :] = jnp.zeros((TAIL, width), jnp.float32)
    for level in range(levels):
        @pl.when(jnp.logical_and(sends(level), me >= 2 ** (level + 1)))
        def _():
            for which in range(2**level):
                map_copy(level, 2**level - 1 - which).start()

        if level > 0:
            @pl.when(me == 2**level - 1)
            def _():
                wait_state()
                forward(held(level - 1), 2**level)

            exclude(level - 1, me, excl, arrived, upper)

        for item in share.get(level, ()):
            sweep(*item)

        @pl.when(jnp.logical_and(upper(level), me >= 2 ** (level + 1)))
        def _():
            map_copy(level, 0).wait_recv()
            arrived[level, pl.ds(width + SENT, TAIL - SENT), :] = jnp.zeros(
                (TAIL - SENT, width), jnp.float32)

            @pl.when(lax.rem(me, 2 ** (level + 1)) == 2 ** (level + 1) - 1)
            def _():
                store(incl.at[level], compose(arrived[level], held(level)[...]))

    @pl.when(me == group - 1)
    def _():
        wait_state()
        forward(held(levels - 1), group)

    exclude(levels - 1, me, excl, arrived, upper)

    @pl.when(jnp.logical_and(forwards, me >= group))
    def _():
        wait_state()
        forward(held(levels), group)

    for item in down[-1:]:
        sweep(*item)

    relays = forwards
    for level in range(levels):
        relays = jnp.logical_or(relays, me == 2**level - 1)

    @pl.when(jnp.logical_not(relays))
    def _():
        wait_state()

    entry = jnp.sum(column(state[0:1, :]) * excl[:width, :], axis=0, keepdims=True)
    entry = entry + excl[width : width + 1, :]
    across = column(entry)
    odd[0:8, :] = jnp.broadcast_to(entry, (8, width))

    def finish(j, _):
        lines = []
        for k in range(8):
            i = j * 8 + k
            line = jnp.sum(across * maps[i, :width, :], axis=0, keepdims=True)
            lines.append(line + maps[i, width : width + 1, :])
        odd[pl.ds(pl.multiple_of(8 + j * 8, 8), 8), :] = jnp.concatenate(lines, axis=0)
        return 0

    lax.fori_loop(0, number // 8, finish, 0)

    before = odd[pl.ds(7, number), :]
    rec = recurrent(before)
    even = pl.ds(0, number, 2)
    upd, cz, cr, cn, off = [coefs[k, even, :] for k in range(5)]
    out[even, :] = (
        upd * before + cz * rec[:, :width] + cr * rec[:, width : 2 * width]
        + cn * rec[:, 2 * width :] + off
    )
    out[pl.ds(1, number, 2), :] = odd[pl.ds(8, number), :]

    @pl.when(me < count - 1)
    def _():
        row_copy().wait_send()

    for level in range(levels):
        @pl.when(jnp.logical_and(sends(level), me >= 2 ** (level + 1)))
        def _():
            for which in range(2**level):
                map_copy(level, which).wait_send()

        @pl.when(me == 2**level - 1)
        def _():
            for which in range(2**level):
                state_copy(which).wait_send()

    @pl.when(forwards)
    def _():
        for which in range(group):
            state_copy(which).wait_send()


def solution(mesh):
    count = mesh.shape["seq"]
    group = 4

    def per_device(inputs, guesses, initial, w_input, w_hidden, biases):
        steps, width = guesses.shape
        levels = int(math.log2(group))
        full = width + TAIL
        line = pltpu.VMEM((steps, width), jnp.float32)
        return pl.pallas_call(
            functools.partial(kernel, count, group),
            out_shape=jax.ShapeDtypeStruct((steps, width), jnp.float32),
            in_specs=[pl.BlockSpec(memory_space=pl.ANY)] * 6,
            out_specs=pl.BlockSpec(memory_space=pltpu.VMEM),
            scratch_shapes=[
                pltpu.VMEM((steps, width), jnp.float32),
                pltpu.VMEM((width,), jnp.float32),
                pltpu.VMEM((width, 3 * width), jnp.float32),
                pltpu.VMEM((width, 3 * width), jnp.float32),
                pltpu.VMEM((3 * width,), jnp.float32),
                pltpu.VMEM((2 * width, 6 * width), jnp.bfloat16),
                pltpu.VMEM((steps // 2, full, width), jnp.float32),
                pltpu.VMEM((steps + 8, width), jnp.float32),
                pltpu.VMEM((8, width), jnp.float32),
                pltpu.VMEM((16, 3 * width), jnp.float32),
                pltpu.VMEM((5, steps, width), jnp.float32),
                pltpu.VMEM((steps // 2 + 8, width), jnp.float32),
                pltpu.VMEM((levels, full, width), jnp.float32),
                pltpu.VMEM((levels, full, width), jnp.float32),
                pltpu.VMEM((full, width), jnp.float32),
                pltpu.VMEM((8, width), jnp.float32),
                pltpu.VMEM((8, width), jnp.float32),
                pltpu.SemaphoreType.DMA((6,)),
                pltpu.SemaphoreType.DMA,
                pltpu.SemaphoreType.DMA,
                pltpu.SemaphoreType.DMA((group - 1,)),
                pltpu.SemaphoreType.DMA((levels,)),
                pltpu.SemaphoreType.DMA((group,)),
                pltpu.SemaphoreType.DMA,
            ],
            compiler_params=pltpu.CompilerParams(
                collective_id=0, has_side_effects=True, vmem_limit_bytes=56 * 2**20),
        )(inputs, guesses, initial, w_input, w_hidden, biases)

    placed = (P(("groups", "seq"), None), P(("groups", "seq"), None), P("groups"), P(), P(), P())
    return jax.shard_map(
        per_device,
        mesh=mesh,
        in_specs=placed,
        out_specs=P(("groups", "seq"), None),
        check_vma=False,
    )
```

```python
import functools

import jax
import jax.numpy as jnp
from jax import lax
from jax.experimental import pallas as pl
from jax.experimental.pallas import tpu as pltpu
from jax.sharding import PartitionSpec as P

TAIL = 16
SENT = 8
BATCH = 4
PAIRS = 3
GROUP = 4


def split(value):
    high = value.astype(jnp.bfloat16)
    low = (value - high.astype(jnp.float32)).astype(jnp.bfloat16)
    return high, low


def product(left, right):
    lh, ll = split(left)
    rh, rl = split(right)
    parts = jnp.concatenate([rh, rl], axis=1)
    both = jnp.dot(
        jnp.concatenate([lh, ll], axis=1),
        jnp.concatenate([parts, parts], axis=0),
        preferred_element_type=jnp.float32,
    )
    width = right.shape[1]
    return both[:, :width] + both[:, width:]


def compose(early, late):
    width = late.shape[1]
    moved = product(early, late[:width])
    return moved[:width], moved[width:] + late[width:]


def column(row):
    width = row.shape[1]
    return jnp.broadcast_to(row, (width, width)).T


def gates(previous, pre, rec):
    width = previous.shape[1]
    pz, pr, pn = (pre[:, :width], pre[:, width : 2 * width], pre[:, 2 * width :])
    cz, cr, cn = (rec[:, :width], rec[:, width : 2 * width], rec[:, 2 * width :])
    update = jax.nn.sigmoid(pz + cz)
    reset = jax.nn.sigmoid(pr + cr)
    cand = jnp.tanh(pn + reset * cn)
    value = (1.0 - update) * cand + update * previous
    coef_update = (previous - cand) * update * (1.0 - update)
    coef_cand = (1.0 - update) * (1.0 - cand * cand) * reset
    coef_reset = (1.0 - update) * (1.0 - cand * cand) * cn * reset * (1.0 - reset)
    offset = value - (update * previous + coef_update * cz + coef_cand * cn + coef_reset * cr)
    return update, coef_update, coef_reset, coef_cand, offset


def store(ref, new):
    width = new[0].shape[0]
    ref[:width, :] = new[0]
    ref[width:, :] = new[1]


def kernel(
    count,
    inputs_hbm, guesses_hbm, initial_hbm, w_input_hbm, w_hidden_hbm, biases_hbm, out,
    inputs, initial, w_input, w_hidden, biases, packed,
    maps, prev, landed, pre_first, coefs, odd, arrived, incl, excl, state, state_next,
    load_sem, row_send, row_recv, map_send, map_recv, state_send, state_recv,
):
    steps, width = inputs.shape
    me = lax.axis_index("seq")
    plane, place = lax.div(me, GROUP), lax.rem(me, GROUP)
    early_plane = plane == 0
    late_plane = me >= count - GROUP
    more = jnp.logical_not(late_plane)
    later_plane = jnp.logical_not(early_plane)
    odd_place = lax.rem(me, 2) == 1
    far = place >= 2
    both = jnp.logical_and

    def row_copy():
        return pltpu.make_async_remote_copy(
            src_ref=prev.at[pl.ds(steps, 8)], dst_ref=landed,
            send_sem=row_send, recv_sem=row_recv, device_id={"seq": me + 1})

    def map_copy(src, slot, sem, device):
        return pltpu.make_async_remote_copy(
            src_ref=src.at[pl.ds(0, width + SENT)],
            dst_ref=arrived.at[slot, pl.ds(0, width + SENT)],
            send_sem=map_send.at[sem], recv_sem=map_recv.at[slot],
            device_id={"seq": device})

    def state_copy(slot, which, device):
        return pltpu.make_async_remote_copy(
            src_ref=state_next.at[slot], dst_ref=state,
            send_sem=state_send.at[slot, which], recv_sem=state_recv,
            device_id={"seq": device})

    total = maps.at[steps // 2 - 1]
    whole_pair = incl.at[0]
    column_next = plane * GROUP + GROUP + jnp.where(far, 2, 0)
    map_copies = [
        (both(jnp.logical_not(odd_place), me > 0), [map_copy(total, 0, 0, me + 1)]),
        (both(me == 2, more), [map_copy(total, 0, 1, 1)]),
        (both(me == 3, more), [map_copy(total, 1, 0, 1)]),
        (both(place == 1, later_plane),
         [map_copy(whole_pair, 1, 0, me + 2), map_copy(whole_pair, 1, 1, me + 1)]),
        (both(both(place == 3, later_plane), more), [map_copy(whole_pair, 1, 0, me - 2)]),
    ]
    state_copies = [
        (me == 0, [state_copy(0, 0, 1)]),
        (me == 1, [state_copy(0, 0, 3), state_copy(0, 1, 2)]),
        (both(odd_place, more),
         [state_copy(1, 0, column_next + 1), state_copy(1, 1, column_next)]),
    ]

    def start(entry):
        @pl.when(entry[0])
        def _():
            for copy in entry[1]:
                copy.start()

    loads = [
        pltpu.make_async_copy(src, dst, load_sem.at[k])
        for k, (src, dst) in enumerate([
            (w_hidden_hbm, w_hidden), (w_input_hbm, w_input),
            (guesses_hbm, prev.at[pl.ds(8, steps)]), (inputs_hbm, inputs),
            (initial_hbm, initial), (biases_hbm, biases)])
    ]
    for load in loads:
        load.start()

    barrier = pltpu.get_barrier_semaphore()

    def here(condition, device):
        @pl.when(condition)
        def _():
            pl.semaphore_signal(barrier, 1, device_id={"seq": device})

    here(me > 0, me - 1)
    here(odd_place, me - 1)
    here(far, plane * GROUP + 1)
    here(both(place == 1, more), me + 2)
    here(both(me == 1, more), 2)
    here(later_plane, plane * GROUP - jnp.where(far, 1, 3))
    arrived[:, width + SENT :, :] = jnp.zeros((2, TAIL - SENT, width), jnp.float32)

    for load in loads:
        load.wait()

    prev[pl.ds(0, 8), :] = jnp.broadcast_to(initial[...][None, :], (8, width))
    high, low = split(w_hidden[...])
    for half in range(2):
        packed[half * width : (half + 1) * width, : 3 * width] = high
        packed[half * width : (half + 1) * width, 3 * width :] = low

    def recurrent(rows):
        both = jnp.dot(
            jnp.concatenate(split(rows), axis=1), packed[...],
            preferred_element_type=jnp.float32)
        return both[:, : 3 * width] + both[:, 3 * width :]

    pre = product(inputs[...], w_input[...]) + biases[...][None, :]
    pre_first[...] = pre[:16]
    previous = prev[pl.ds(7, steps), :]
    for k, part in enumerate(gates(previous, pre, recurrent(previous))):
        coefs[k] = part

    copies = jnp.int32(1)
    for condition, some in map_copies + state_copies:
        copies += len(some) * condition.astype(jnp.int32)

    @pl.when(me < count - 1)
    def _():
        pl.semaphore_wait(barrier, copies)
        row_copy().start()

    rows = lax.broadcasted_iota(jnp.int32, (width, width), 0)
    cols = lax.broadcasted_iota(jnp.int32, (width, width), 1)
    top = lax.broadcasted_iota(jnp.int32, (TAIL, width), 0) == 0

    def step_map(t):
        one = pl.ds(t, 1)
        upd, cz, cr, cn, off = [coefs[k, one, :] for k in range(5)]
        body = (
            jnp.where(rows == cols, upd, 0.0)
            + cz * w_hidden[:, :width]
            + cr * w_hidden[:, width : 2 * width]
            + cn * w_hidden[:, 2 * width :]
        )
        return jnp.concatenate([body, jnp.where(top, off, 0.0)], axis=0)

    def pair(i):
        store(maps.at[i], compose(step_map(2 * i), step_map(2 * i + 1)))

    def pairs(start, size):
        news = [compose(step_map(2 * i), step_map(2 * i + 1))
                for i in [start + k for k in range(size)]]
        for k, new in enumerate(news):
            store(maps.at[start + k], new)

    def pairs_body(j, _):
        pairs(1 + PAIRS * j, PAIRS)
        return 0

    number = steps // 2
    whole = (number - 1) // PAIRS
    lax.fori_loop(0, whole, pairs_body, 0)

    @pl.when(me > 0)
    def _():
        row_copy().wait_recv()
        prev[pl.ds(7, 1), :] = landed[pl.ds(7, 1), :]
        fixed = prev[pl.ds(7, 16), :]
        for k, part in enumerate(gates(fixed, pre_first[...], recurrent(fixed))):
            coefs[k, :16, :] = part

    for i in [0] + list(range(1 + PAIRS * whole, number)):
        pair(i)

    def sweep(first, stride, distance, number):
        batch = min(BATCH, number)

        def some(start, size):
            where = [start + stride * j for j in range(size)]
            news = [compose(maps[i - distance], maps[i]) for i in where]
            for i, new in zip(where, news):
                store(maps.at[i], new)

        def body(j, _):
            some(first + j * (stride * batch), batch)
            return 0

        whole = number // batch
        if whole > 1:
            lax.fori_loop(0, whole, body, 0)
        else:
            some(first, batch)
        if number % batch:
            some(first + whole * batch * stride, number % batch)

    distance = 1
    while distance < number:
        sweep(2 * distance - 1, 2 * distance, distance, number // (2 * distance))
        distance *= 2

    down = []
    distance = number // 4
    while distance >= 1:
        down.append((3 * distance - 1, 2 * distance, distance, number // (2 * distance) - 1))
        distance //= 2

    def applied(row, ref):
        moved = jnp.sum(column(row) * ref[:width, :], axis=0, keepdims=True)
        return moved + ref[width : width + 1, :]

    def arrival(slot):
        map_copy(total, slot, 0, me + 1).wait_recv()

    def wait_state():
        state_copy(0, 0, me + 1).wait_recv()

    @pl.when(me == 0)
    def _():
        state[...] = jnp.broadcast_to(initial[...][None, :], state.shape)
        state_next[0] = jnp.broadcast_to(applied(state[0:1, :], total), (8, width))

    start(state_copies[0])
    for entry in map_copies[:3]:
        start(entry)
    excl[:width, :] = jnp.where(rows == cols, 1.0, 0.0)
    excl[width:, :] = jnp.zeros((TAIL, width), jnp.float32)
    for item in down[:-2]:
        sweep(*item)

    @pl.when(me == 1)
    def _():
        wait_state()
        state_next[0] = jnp.broadcast_to(applied(state[0:1, :], total), (8, width))

    start(state_copies[1])

    @pl.when(both(odd_place, me >= 3))
    def _():
        arrival(0)
        store(incl.at[0], compose(arrived[0], total[...]))
        excl[...] = arrived[0]

    for entry in map_copies[3:]:
        start(entry)
    for item in down[-2:-1]:
        sweep(*item)

    @pl.when(both(me == 1, more))
    def _():
        arrival(0)
        arrival(1)
        state_next[1] = jnp.broadcast_to(
            applied(applied(state_next[0, 0:1, :], arrived.at[0]), arrived.at[1]), (8, width))

    @pl.when(me == 3)
    def _():
        wait_state()
        state_next[1] = jnp.broadcast_to(applied(state[0:1, :], whole_pair), (8, width))

    @pl.when(both(later_plane, jnp.logical_or(far, both(place == 1, more))))
    def _():
        arrival(1)

    @pl.when(both(both(later_plane, more), place == 1))
    def _():
        store(incl.at[1], compose(incl[0], arrived[1]))

    @pl.when(both(both(later_plane, more), place == 3))
    def _():
        store(incl.at[1], compose(arrived[1], incl[0]))

    @pl.when(both(both(later_plane, more), odd_place))
    def _():
        wait_state()
        state_next[1] = jnp.broadcast_to(applied(state[0:1, :], incl.at[1]), (8, width))

    start(state_copies[2])

    @pl.when(both(later_plane, place == 2))
    def _():
        excl[...] = arrived[1]

    @pl.when(both(later_plane, place == 3))
    def _():
        store(excl, compose(arrived[1], arrived[0]))

    for item in down[-1:]:
        sweep(*item)

    @pl.when(jnp.logical_or(
        me == 2, both(later_plane, jnp.logical_or(late_plane, jnp.logical_not(odd_place)))))
    def _():
        wait_state()

    entry = applied(state[0:1, :], excl)
    across = column(entry)
    odd[0:8, :] = jnp.broadcast_to(entry, (8, width))

    def finish(j, _):
        lines = []
        for k in range(8):
            i = j * 8 + k
            line = jnp.sum(across * maps[i, :width, :], axis=0, keepdims=True)
            lines.append(line + maps[i, width : width + 1, :])
        odd[pl.ds(pl.multiple_of(8 + j * 8, 8), 8), :] = jnp.concatenate(lines, axis=0)
        return 0

    lax.fori_loop(0, number // 8, finish, 0)

    before = odd[pl.ds(7, number), :]
    rec = recurrent(before)
    even = pl.ds(0, number, 2)
    upd, cz, cr, cn, off = [coefs[k, even, :] for k in range(5)]
    out[even, :] = (
        upd * before + cz * rec[:, :width] + cr * rec[:, width : 2 * width]
        + cn * rec[:, 2 * width :] + off
    )
    out[pl.ds(1, number, 2), :] = odd[pl.ds(8, number), :]

    @pl.when(me < count - 1)
    def _():
        row_copy().wait_send()

    for condition, some in map_copies + state_copies:
        @pl.when(condition)
        def _():
            for copy in some:
                copy.wait_send()


def solution(mesh):
    count = mesh.shape["seq"]

    def per_device(inputs, guesses, initial, w_input, w_hidden, biases):
        steps, width = guesses.shape
        full = width + TAIL
        line = pltpu.VMEM((steps, width), jnp.float32)
        return pl.pallas_call(
            functools.partial(kernel, count),
            out_shape=jax.ShapeDtypeStruct((steps, width), jnp.float32),
            in_specs=[pl.BlockSpec(memory_space=pl.ANY)] * 6,
            out_specs=pl.BlockSpec(memory_space=pltpu.VMEM),
            scratch_shapes=[
                pltpu.VMEM((steps, width), jnp.float32),
                pltpu.VMEM((width,), jnp.float32),
                pltpu.VMEM((width, 3 * width), jnp.float32),
                pltpu.VMEM((width, 3 * width), jnp.float32),
                pltpu.VMEM((3 * width,), jnp.float32),
                pltpu.VMEM((2 * width, 6 * width), jnp.bfloat16),
                pltpu.VMEM((steps // 2, full, width), jnp.float32),
                pltpu.VMEM((steps + 8, width), jnp.float32),
                pltpu.VMEM((8, width), jnp.float32),
                pltpu.VMEM((16, 3 * width), jnp.float32),
                pltpu.VMEM((5, steps, width), jnp.float32),
                pltpu.VMEM((steps // 2 + 8, width), jnp.float32),
                pltpu.VMEM((2, full, width), jnp.float32),
                pltpu.VMEM((2, full, width), jnp.float32),
                pltpu.VMEM((full, width), jnp.float32),
                pltpu.VMEM((8, width), jnp.float32),
                pltpu.VMEM((2, 8, width), jnp.float32),
                pltpu.SemaphoreType.DMA((6,)),
                pltpu.SemaphoreType.DMA,
                pltpu.SemaphoreType.DMA,
                pltpu.SemaphoreType.DMA((2,)),
                pltpu.SemaphoreType.DMA((2,)),
                pltpu.SemaphoreType.DMA((2, 2)),
                pltpu.SemaphoreType.DMA,
            ],
            compiler_params=pltpu.CompilerParams(
                collective_id=0, has_side_effects=True, vmem_limit_bytes=56 * 2**20),
        )(inputs, guesses, initial, w_input, w_hidden, biases)

    placed = (P(("groups", "seq"), None), P(("groups", "seq"), None), P("groups"), P(), P(), P())
    return jax.shard_map(
        per_device,
        mesh=mesh,
        in_specs=placed,
        out_specs=P(("groups", "seq"), None),
        check_vma=False,
    )
```

```python
import functools

import jax
import jax.numpy as jnp
from jax import lax
from jax.experimental import pallas as pl
from jax.experimental.pallas import tpu as pltpu
from jax.sharding import PartitionSpec as P

TAIL = 16
SENT = 8
BATCH = 16
PAIRS = 8
GROUP = 4


def split(value):
    high = value.astype(jnp.bfloat16)
    low = (value - high.astype(jnp.float32)).astype(jnp.bfloat16)
    return high, low


def product(left, right):
    lh, ll = split(left)
    rh, rl = split(right)
    parts = jnp.concatenate([rh, rl], axis=1)
    both = jnp.dot(
        jnp.concatenate([lh, ll], axis=1),
        jnp.concatenate([parts, parts], axis=0),
        preferred_element_type=jnp.float32,
    )
    width = right.shape[1]
    return both[:, :width] + both[:, width:]


def compose(early, late):
    width = late.shape[1]
    moved = product(early, late[:width])
    return moved[:width], moved[width:] + late[width:]


def column(row):
    width = row.shape[1]
    return jnp.broadcast_to(row, (width, width)).T


def gates(previous, pre, rec):
    width = previous.shape[1]
    pz, pr, pn = (pre[:, :width], pre[:, width : 2 * width], pre[:, 2 * width :])
    cz, cr, cn = (rec[:, :width], rec[:, width : 2 * width], rec[:, 2 * width :])
    update = jax.nn.sigmoid(pz + cz)
    reset = jax.nn.sigmoid(pr + cr)
    cand = jnp.tanh(pn + reset * cn)
    value = (1.0 - update) * cand + update * previous
    coef_update = (previous - cand) * update * (1.0 - update)
    coef_cand = (1.0 - update) * (1.0 - cand * cand) * reset
    coef_reset = (1.0 - update) * (1.0 - cand * cand) * cn * reset * (1.0 - reset)
    offset = value - (update * previous + coef_update * cz + coef_cand * cn + coef_reset * cr)
    return update, coef_update, coef_reset, coef_cand, offset


def store(ref, new):
    width = new[0].shape[0]
    ref[:width, :] = new[0]
    ref[width:, :] = new[1]


def kernel(
    count,
    inputs_hbm, guesses_hbm, initial_hbm, w_input_hbm, w_hidden_hbm, biases_hbm, out,
    inputs, initial, w_input, w_hidden, biases, packed,
    maps, prev, landed, pre_first, coefs, odd, arrived, incl, excl, state, state_next,
    load_sem, row_send, row_recv, map_send, map_recv, state_send, state_recv,
):
    steps, width = inputs.shape
    me = lax.axis_index("seq")
    plane, place = lax.div(me, GROUP), lax.rem(me, GROUP)
    early_plane = plane == 0
    late_plane = me >= count - GROUP
    more = jnp.logical_not(late_plane)
    later_plane = jnp.logical_not(early_plane)
    odd_place = lax.rem(me, 2) == 1
    far = place >= 2
    both = jnp.logical_and

    def row_copy():
        return pltpu.make_async_remote_copy(
            src_ref=prev.at[pl.ds(steps, 8)], dst_ref=landed,
            send_sem=row_send, recv_sem=row_recv, device_id={"seq": me + 1})

    def map_copy(src, slot, sem, device):
        return pltpu.make_async_remote_copy(
            src_ref=src.at[pl.ds(0, width + SENT)],
            dst_ref=arrived.at[slot, pl.ds(0, width + SENT)],
            send_sem=map_send.at[sem], recv_sem=map_recv.at[slot],
            device_id={"seq": device})

    def state_copy(slot, which, device):
        return pltpu.make_async_remote_copy(
            src_ref=state_next.at[slot], dst_ref=state,
            send_sem=state_send.at[slot, which], recv_sem=state_recv,
            device_id={"seq": device})

    total = maps.at[steps // 2 - 1]
    whole_pair = incl.at[0]
    column_next = plane * GROUP + GROUP + jnp.where(far, 2, 0)
    map_copies = [
        (both(jnp.logical_not(odd_place), me > 0), [map_copy(total, 0, 0, me + 1)]),
        (both(place == 1, later_plane),
         [map_copy(whole_pair, 1, 0, me + 2), map_copy(whole_pair, 1, 1, me + 1)]),
        (both(both(place == 3, later_plane), more), [map_copy(whole_pair, 1, 0, me - 2)]),
    ]
    state_copies = [
        (me == 0, [state_copy(0, 0, 1)]),
        (me == 1, [state_copy(0, 0, 3), state_copy(0, 1, 2)]),
        (both(both(odd_place, more), me >= 3),
         [state_copy(1, 0, column_next + 1), state_copy(1, 1, column_next)]),
        (both(me == 3, more), [state_copy(1, 2, GROUP), state_copy(1, 3, GROUP + 1)]),
    ]

    def start(entry):
        @pl.when(entry[0])
        def _():
            for copy in entry[1]:
                copy.start()

    loads = [
        pltpu.make_async_copy(src, dst, load_sem.at[k])
        for k, (src, dst) in enumerate([
            (guesses_hbm, prev.at[pl.ds(8, steps)]), (initial_hbm, initial),
            (w_hidden_hbm, w_hidden), (inputs_hbm, inputs),
            (w_input_hbm, w_input), (biases_hbm, biases)])
    ]
    for load in loads:
        load.start()

    barrier = pltpu.get_barrier_semaphore()

    def here(condition, device):
        @pl.when(condition)
        def _():
            pl.semaphore_signal(barrier, 1, device_id={"seq": device})

    here(me > 0, me - 1)
    here(odd_place, me - 1)
    here(far, plane * GROUP + 1)
    here(both(both(place == 1, later_plane), more), me + 2)
    here(later_plane, plane * GROUP - jnp.where(jnp.logical_or(far, plane == 1), 1, 3))
    arrived[:, width + SENT :, :] = jnp.zeros((2, TAIL - SENT, width), jnp.float32)

    for load in loads[:3]:
        load.wait()

    prev[pl.ds(0, 8), :] = jnp.broadcast_to(initial[...][None, :], (8, width))
    high, low = split(w_hidden[...])
    for half in range(2):
        packed[half * width : (half + 1) * width, : 3 * width] = high
        packed[half * width : (half + 1) * width, 3 * width :] = low

    def recurrent(rows):
        both = jnp.dot(
            jnp.concatenate(split(rows), axis=1), packed[...],
            preferred_element_type=jnp.float32)
        return both[:, : 3 * width] + both[:, 3 * width :]

    previous = prev[pl.ds(7, steps), :]
    rec = recurrent(previous)
    for load in loads[3:]:
        load.wait()
    pre = product(inputs[...], w_input[...]) + biases[...][None, :]
    pre_first[...] = pre[:16]
    for k, part in enumerate(gates(previous, pre, rec)):
        coefs[k] = part

    copies = jnp.int32(1)
    for condition, some in map_copies + state_copies:
        copies += len(some) * condition.astype(jnp.int32)

    @pl.when(me < count - 1)
    def _():
        pl.semaphore_wait(barrier, copies)
        row_copy().start()

    rows = lax.broadcasted_iota(jnp.int32, (width, width), 0)
    cols = lax.broadcasted_iota(jnp.int32, (width, width), 1)
    top = lax.broadcasted_iota(jnp.int32, (TAIL, width), 0) == 0

    def step_map(t):
        one = pl.ds(t, 1)
        upd, cz, cr, cn, off = [coefs[k, one, :] for k in range(5)]
        body = (
            jnp.where(rows == cols, upd, 0.0)
            + cz * w_hidden[:, :width]
            + cr * w_hidden[:, width : 2 * width]
            + cn * w_hidden[:, 2 * width :]
        )
        return jnp.concatenate([body, jnp.where(top, off, 0.0)], axis=0)

    def pairs(start, size):
        news = [compose(step_map(2 * i), step_map(2 * i + 1))
                for i in [start + k for k in range(size)]]
        for k, new in enumerate(news):
            store(maps.at[start + k], new)

    def pairs_body(j, _):
        pairs(PAIRS * j, PAIRS)
        return 0

    number = steps // 2
    lax.fori_loop(1, number // PAIRS, pairs_body, 0)

    @pl.when(me > 0)
    def _():
        row_copy().wait_recv()
        prev[pl.ds(7, 1), :] = landed[pl.ds(7, 1), :]
        fixed = prev[pl.ds(7, 16), :]
        for k, part in enumerate(gates(fixed, pre_first[...], recurrent(fixed))):
            coefs[k, :16, :] = part

    pairs(0, PAIRS)

    def sweep(first, stride, distance, number):
        batch = min(BATCH, number)

        def some(start, size):
            where = [start + stride * j for j in range(size)]
            news = [compose(maps[i - distance], maps[i]) for i in where]
            for i, new in zip(where, news):
                store(maps.at[i], new)

        def body(j, _):
            some(first + j * (stride * batch), batch)
            return 0

        whole = number // batch
        if whole > 1:
            lax.fori_loop(0, whole, body, 0)
        else:
            some(first, batch)
        if number % batch:
            some(first + whole * batch * stride, number % batch)

    distance = 1
    while distance < number:
        sweep(2 * distance - 1, 2 * distance, distance, number // (2 * distance))
        distance *= 2

    down = []
    distance = number // 4
    while distance >= 1:
        down.append((3 * distance - 1, 2 * distance, distance, number // (2 * distance) - 1))
        distance //= 2

    def applied(row, ref):
        moved = jnp.sum(column(row) * ref[:width, :], axis=0, keepdims=True)
        return moved + ref[width : width + 1, :]

    def arrival(slot):
        map_copy(total, slot, 0, me + 1).wait_recv()

    def wait_state():
        state_copy(0, 0, me + 1).wait_recv()

    @pl.when(me == 0)
    def _():
        state[...] = jnp.broadcast_to(initial[...][None, :], state.shape)
        state_next[0] = jnp.broadcast_to(applied(state[0:1, :], total), (8, width))

    start(state_copies[0])
    start(map_copies[0])
    excl[:width, :] = jnp.where(rows == cols, 1.0, 0.0)
    excl[width:, :] = jnp.zeros((TAIL, width), jnp.float32)
    for item in down[:-2]:
        sweep(*item)

    @pl.when(me == 1)
    def _():
        wait_state()
        state_next[0] = jnp.broadcast_to(applied(state[0:1, :], total), (8, width))

    start(state_copies[1])

    @pl.when(both(odd_place, me >= 3))
    def _():
        arrival(0)
        store(incl.at[0], compose(arrived[0], total[...]))
        excl[...] = arrived[0]

    for entry in map_copies[1:]:
        start(entry)
    for item in down[-2:-1]:
        sweep(*item)

    @pl.when(me == 3)
    def _():
        wait_state()
        state_next[1] = jnp.broadcast_to(applied(state[0:1, :], whole_pair), (8, width))

    @pl.when(both(later_plane, jnp.logical_or(far, both(place == 1, more))))
    def _():
        arrival(1)

    @pl.when(both(both(later_plane, more), place == 1))
    def _():
        store(incl.at[1], compose(incl[0], arrived[1]))

    @pl.when(both(both(later_plane, more), place == 3))
    def _():
        store(incl.at[1], compose(arrived[1], incl[0]))

    @pl.when(both(both(later_plane, more), odd_place))
    def _():
        wait_state()
        state_next[1] = jnp.broadcast_to(applied(state[0:1, :], incl.at[1]), (8, width))

    start(state_copies[2])
    start(state_copies[3])

    @pl.when(both(later_plane, place == 2))
    def _():
        excl[...] = arrived[1]

    @pl.when(both(later_plane, place == 3))
    def _():
        store(excl, compose(arrived[1], arrived[0]))

    for item in down[-1:]:
        sweep(*item)

    @pl.when(jnp.logical_or(
        me == 2, both(later_plane, jnp.logical_or(late_plane, jnp.logical_not(odd_place)))))
    def _():
        wait_state()

    entry = applied(state[0:1, :], excl)
    across = column(entry)
    odd[0:8, :] = jnp.broadcast_to(entry, (8, width))

    def finish(j, _):
        lines = []
        for k in range(8):
            i = j * 8 + k
            line = jnp.sum(across * maps[i, :width, :], axis=0, keepdims=True)
            lines.append(line + maps[i, width : width + 1, :])
        odd[pl.ds(pl.multiple_of(8 + j * 8, 8), 8), :] = jnp.concatenate(lines, axis=0)
        return 0

    lax.fori_loop(0, number // 8, finish, 0)

    before = odd[pl.ds(7, number), :]
    rec = recurrent(before)
    even = pl.ds(0, number, 2)
    upd, cz, cr, cn, off = [coefs[k, even, :] for k in range(5)]
    out[even, :] = (
        upd * before + cz * rec[:, :width] + cr * rec[:, width : 2 * width]
        + cn * rec[:, 2 * width :] + off
    )
    out[pl.ds(1, number, 2), :] = odd[pl.ds(8, number), :]

    @pl.when(me < count - 1)
    def _():
        row_copy().wait_send()

    for condition, some in map_copies + state_copies:
        @pl.when(condition)
        def _():
            for copy in some:
                copy.wait_send()


def solution(mesh):
    count = mesh.shape["seq"]

    def per_device(inputs, guesses, initial, w_input, w_hidden, biases):
        steps, width = guesses.shape
        full = width + TAIL
        line = pltpu.VMEM((steps, width), jnp.float32)
        return pl.pallas_call(
            functools.partial(kernel, count),
            out_shape=jax.ShapeDtypeStruct((steps, width), jnp.float32),
            in_specs=[pl.BlockSpec(memory_space=pl.ANY)] * 6,
            out_specs=pl.BlockSpec(memory_space=pltpu.VMEM),
            scratch_shapes=[
                pltpu.VMEM((steps, width), jnp.float32),
                pltpu.VMEM((width,), jnp.float32),
                pltpu.VMEM((width, 3 * width), jnp.float32),
                pltpu.VMEM((width, 3 * width), jnp.float32),
                pltpu.VMEM((3 * width,), jnp.float32),
                pltpu.VMEM((2 * width, 6 * width), jnp.bfloat16),
                pltpu.VMEM((steps // 2, full, width), jnp.float32),
                pltpu.VMEM((steps + 8, width), jnp.float32),
                pltpu.VMEM((8, width), jnp.float32),
                pltpu.VMEM((16, 3 * width), jnp.float32),
                pltpu.VMEM((5, steps, width), jnp.float32),
                pltpu.VMEM((steps // 2 + 8, width), jnp.float32),
                pltpu.VMEM((2, full, width), jnp.float32),
                pltpu.VMEM((2, full, width), jnp.float32),
                pltpu.VMEM((full, width), jnp.float32),
                pltpu.VMEM((8, width), jnp.float32),
                pltpu.VMEM((2, 8, width), jnp.float32),
                pltpu.SemaphoreType.DMA((6,)),
                pltpu.SemaphoreType.DMA,
                pltpu.SemaphoreType.DMA,
                pltpu.SemaphoreType.DMA((2,)),
                pltpu.SemaphoreType.DMA((2,)),
                pltpu.SemaphoreType.DMA((2, 4)),
                pltpu.SemaphoreType.DMA,
            ],
            compiler_params=pltpu.CompilerParams(
                collective_id=0, has_side_effects=True, vmem_limit_bytes=56 * 2**20),
        )(inputs, guesses, initial, w_input, w_hidden, biases)

    placed = (P(("groups", "seq"), None), P(("groups", "seq"), None), P("groups"), P(), P(), P())
    return jax.shard_map(
        per_device,
        mesh=mesh,
        in_specs=placed,
        out_specs=P(("groups", "seq"), None),
        check_vma=False,
    )
```

```python
import functools

import jax
import jax.numpy as jnp
from jax import lax
from jax.experimental import pallas as pl
from jax.experimental.pallas import tpu as pltpu
from jax.sharding import PartitionSpec as P

TAIL = 16
SENT = 8
BATCH = 16
PAIRS = 8
GROUP = 4


def split(value):
    high = value.astype(jnp.bfloat16)
    low = (value - high.astype(jnp.float32)).astype(jnp.bfloat16)
    return high, low


def product(left, right):
    lh, ll = split(left)
    rh, rl = split(right)
    parts = jnp.concatenate([rh, rl], axis=1)
    both = jnp.dot(
        jnp.concatenate([lh, ll], axis=1),
        jnp.concatenate([parts, parts], axis=0),
        preferred_element_type=jnp.float32,
    )
    width = right.shape[1]
    return both[:, :width] + both[:, width:]


def compose(early, late):
    width = late.shape[1]
    moved = product(early, late[:width])
    return moved[:width], moved[width:] + late[width:]


def column(row):
    width = row.shape[1]
    return jnp.broadcast_to(row, (width, width)).T


def gates(previous, pre, rec):
    width = previous.shape[1]
    pz, pr, pn = (pre[:, :width], pre[:, width : 2 * width], pre[:, 2 * width :])
    cz, cr, cn = (rec[:, :width], rec[:, width : 2 * width], rec[:, 2 * width :])
    update = jax.nn.sigmoid(pz + cz)
    reset = jax.nn.sigmoid(pr + cr)
    cand = jnp.tanh(pn + reset * cn)
    value = (1.0 - update) * cand + update * previous
    coef_update = (previous - cand) * update * (1.0 - update)
    coef_cand = (1.0 - update) * (1.0 - cand * cand) * reset
    coef_reset = (1.0 - update) * (1.0 - cand * cand) * cn * reset * (1.0 - reset)
    offset = value - (update * previous + coef_update * cz + coef_cand * cn + coef_reset * cr)
    return update, coef_update, coef_reset, coef_cand, offset


def store(ref, new):
    width = new[0].shape[0]
    ref[:width, :] = new[0]
    ref[width:, :] = new[1]


def kernel(
    count,
    inputs_hbm, guesses_hbm, initial_hbm, w_input_hbm, w_hidden_hbm, biases_hbm, out,
    inputs, initial, w_input, w_hidden, biases, packed,
    maps, prev, landed, pre_first, coefs, odd, arrived, incl, excl, state, state_next,
    load_sem, row_send, row_recv, map_send, map_recv, state_send, state_recv,
):
    steps, width = inputs.shape
    me = lax.axis_index("seq")
    plane, place = lax.div(me, GROUP), lax.rem(me, GROUP)
    early_plane = plane == 0
    late_plane = me >= count - GROUP
    more = jnp.logical_not(late_plane)
    later_plane = jnp.logical_not(early_plane)
    odd_place = lax.rem(me, 2) == 1
    far = place >= 2
    both = jnp.logical_and

    def row_copy():
        return pltpu.make_async_remote_copy(
            src_ref=prev.at[pl.ds(steps, 8)], dst_ref=landed,
            send_sem=row_send, recv_sem=row_recv, device_id={"seq": me + 1})

    def map_copy(src, slot, sem, device):
        return pltpu.make_async_remote_copy(
            src_ref=src.at[pl.ds(0, width + SENT)],
            dst_ref=arrived.at[slot, pl.ds(0, width + SENT)],
            send_sem=map_send.at[sem], recv_sem=map_recv.at[slot],
            device_id={"seq": device})

    def state_copy(slot, which, device):
        return pltpu.make_async_remote_copy(
            src_ref=state_next.at[slot], dst_ref=state,
            send_sem=state_send.at[slot, which], recv_sem=state_recv,
            device_id={"seq": device})

    total = maps.at[steps // 2 - 1]
    whole_pair = incl.at[0]
    column_next = plane * GROUP + GROUP + jnp.where(far, 2, 0)
    map_copies = [
        (both(jnp.logical_not(odd_place), me > 0), [map_copy(total, 0, 0, me + 1)]),
        (both(place == 1, later_plane),
         [map_copy(whole_pair, 1, 0, me + 2)]),
        (both(both(place == 3, later_plane), more), [map_copy(whole_pair, 1, 0, me - 2)]),
        (both(place == 3, later_plane), [map_copy(arrived.at[1], 1, 1, me - 1)]),
    ]
    state_copies = [
        (me == 0, [state_copy(0, 0, 1)]),
        (me == 1, [state_copy(0, 0, 3), state_copy(0, 1, 2)]),
        (both(both(odd_place, more), me >= 3),
         [state_copy(1, 0, column_next + 1), state_copy(1, 1, column_next)]),
        (both(me == 3, more), [state_copy(1, 2, GROUP), state_copy(1, 3, GROUP + 1)]),
    ]

    def start(entry):
        @pl.when(entry[0])
        def _():
            for copy in entry[1]:
                copy.start()

    loads = [
        pltpu.make_async_copy(src, dst, load_sem.at[k])
        for k, (src, dst) in enumerate([
            (guesses_hbm, prev.at[pl.ds(8, steps)]), (initial_hbm, initial),
            (w_hidden_hbm, w_hidden), (inputs_hbm, inputs),
            (w_input_hbm, w_input), (biases_hbm, biases)])
    ]
    for load in loads:
        load.start()

    barrier = pltpu.get_barrier_semaphore()

    def here(condition, device):
        @pl.when(condition)
        def _():
            pl.semaphore_signal(barrier, 1, device_id={"seq": device})

    here(me > 0, me - 1)
    here(odd_place, me - 1)
    here(far, plane * GROUP + jnp.where(both(later_plane, place == 2), 3, 1))
    here(both(both(place == 1, later_plane), more), me + 2)
    here(later_plane, plane * GROUP - jnp.where(jnp.logical_or(far, plane == 1), 1, 3))
    arrived[:, width + SENT :, :] = jnp.zeros((2, TAIL - SENT, width), jnp.float32)

    for load in loads[:3]:
        load.wait()

    prev[pl.ds(0, 8), :] = jnp.broadcast_to(initial[...][None, :], (8, width))
    high, low = split(w_hidden[...])
    for half in range(2):
        packed[half * width : (half + 1) * width, : 3 * width] = high
        packed[half * width : (half + 1) * width, 3 * width :] = low

    def recurrent(rows):
        both = jnp.dot(
            jnp.concatenate(split(rows), axis=1), packed[...],
            preferred_element_type=jnp.float32)
        return both[:, : 3 * width] + both[:, 3 * width :]

    previous = prev[pl.ds(7, steps), :]
    rec = recurrent(previous)
    for load in loads[3:]:
        load.wait()
    pre = product(inputs[...], w_input[...]) + biases[...][None, :]
    pre_first[...] = pre[:16]
    for k, part in enumerate(gates(previous, pre, rec)):
        coefs[k] = part

    copies = (me < count - 1).astype(jnp.int32)
    for condition, some in map_copies + state_copies:
        copies += len(some) * condition.astype(jnp.int32)

    pl.semaphore_wait(barrier, copies)

    @pl.when(me < count - 1)
    def _():
        row_copy().start()

    rows = lax.broadcasted_iota(jnp.int32, (width, width), 0)
    cols = lax.broadcasted_iota(jnp.int32, (width, width), 1)
    top = lax.broadcasted_iota(jnp.int32, (TAIL, width), 0) == 0

    def step_map(t):
        one = pl.ds(t, 1)
        upd, cz, cr, cn, off = [coefs[k, one, :] for k in range(5)]
        body = (
            jnp.where(rows == cols, upd, 0.0)
            + cz * w_hidden[:, :width]
            + cr * w_hidden[:, width : 2 * width]
            + cn * w_hidden[:, 2 * width :]
        )
        return jnp.concatenate([body, jnp.where(top, off, 0.0)], axis=0)

    def pairs(start, size):
        news = [compose(step_map(2 * i), step_map(2 * i + 1))
                for i in [start + k for k in range(size)]]
        for k, new in enumerate(news):
            store(maps.at[start + k], new)

    number = steps // 2
    for k in range(2):
        pairs(PAIRS + k * (number - PAIRS) // 2, (number - PAIRS) // 2)

    @pl.when(me > 0)
    def _():
        row_copy().wait_recv()
        prev[pl.ds(7, 1), :] = landed[pl.ds(7, 1), :]
        fixed = prev[pl.ds(7, 16), :]
        for k, part in enumerate(gates(fixed, pre_first[...], recurrent(fixed))):
            coefs[k, :16, :] = part

    pairs(0, PAIRS)

    def sweep(first, stride, distance, number):
        batch = min(BATCH, number)

        def some(start, size):
            where = [start + stride * j for j in range(size)]
            news = [compose(maps[i - distance], maps[i]) for i in where]
            for i, new in zip(where, news):
                store(maps.at[i], new)

        def body(j, _):
            some(first + j * (stride * batch), batch)
            return 0

        whole = number // batch
        if whole > 1:
            lax.fori_loop(0, whole, body, 0)
        else:
            some(first, batch)
        if number % batch:
            some(first + whole * batch * stride, number % batch)

    distance = 1
    while distance < number:
        sweep(2 * distance - 1, 2 * distance, distance, number // (2 * distance))
        distance *= 2

    down = []
    distance = number // 4
    while distance >= 1:
        down.append((3 * distance - 1, 2 * distance, distance, number // (2 * distance) - 1))
        distance //= 2

    def applied(row, ref):
        moved = jnp.sum(column(row) * ref[:width, :], axis=0, keepdims=True)
        return moved + ref[width : width + 1, :]

    def arrival(slot):
        map_copy(total, slot, 0, me + 1).wait_recv()

    def wait_state():
        state_copy(0, 0, me + 1).wait_recv()

    @pl.when(me == 0)
    def _():
        state[...] = jnp.broadcast_to(initial[...][None, :], state.shape)
        state_next[0] = jnp.broadcast_to(applied(state[0:1, :], total), (8, width))

    start(state_copies[0])
    start(map_copies[0])
    excl[:width, :] = jnp.where(rows == cols, 1.0, 0.0)
    excl[width:, :] = jnp.zeros((TAIL, width), jnp.float32)
    for item in down[:-2]:
        sweep(*item)

    @pl.when(me == 1)
    def _():
        wait_state()
        state_next[0] = jnp.broadcast_to(applied(state[0:1, :], total), (8, width))

    start(state_copies[1])

    @pl.when(both(odd_place, me >= 3))
    def _():
        arrival(0)
        store(incl.at[0], compose(arrived[0], total[...]))
        excl[...] = arrived[0]

    for entry in map_copies[1:3]:
        start(entry)
    for item in down[-2:-1]:
        sweep(*item)

    @pl.when(me == 3)
    def _():
        wait_state()
        state_next[1] = jnp.broadcast_to(applied(state[0:1, :], whole_pair), (8, width))

    @pl.when(both(later_plane, jnp.logical_or(far, both(place == 1, more))))
    def _():
        arrival(1)

    start(map_copies[3])
    second = both(both(plane == 1, more), place == 3)

    @pl.when(both(both(later_plane, more), place == 1))
    def _():
        store(incl.at[1], compose(incl[0], arrived[1]))

    @pl.when(both(both(plane > 1, more), place == 3))
    def _():
        store(incl.at[1], compose(arrived[1], incl[0]))

    @pl.when(second)
    def _():
        wait_state()
        row = applied(applied(state[0:1, :], arrived.at[1]), whole_pair)
        state_next[1] = jnp.broadcast_to(row, (8, width))

    @pl.when(both(both(both(later_plane, more), odd_place), jnp.logical_not(second)))
    def _():
        wait_state()
        state_next[1] = jnp.broadcast_to(applied(state[0:1, :], incl.at[1]), (8, width))

    start(state_copies[2])
    start(state_copies[3])

    @pl.when(both(later_plane, place == 2))
    def _():
        excl[...] = arrived[1]

    @pl.when(both(later_plane, place == 3))
    def _():
        store(excl, compose(arrived[1], arrived[0]))

    for item in down[-1:]:
        sweep(*item)

    @pl.when(jnp.logical_or(
        me == 2, both(later_plane, jnp.logical_or(late_plane, jnp.logical_not(odd_place)))))
    def _():
        wait_state()

    entry = applied(state[0:1, :], excl)
    across = column(entry)
    odd[0:8, :] = jnp.broadcast_to(entry, (8, width))

    for j in range(0, number, 8):
        lines = []
        for i in range(j, j + 8):
            line = jnp.sum(across * maps[i, :width, :], axis=0, keepdims=True)
            lines.append(line + maps[i, width : width + 1, :])
        odd[j + 8 : j + 16, :] = jnp.concatenate(lines, axis=0)

    before = odd[pl.ds(7, number), :]
    rec = recurrent(before)
    even = pl.ds(0, number, 2)
    upd, cz, cr, cn, off = [coefs[k, even, :] for k in range(5)]
    out[even, :] = (
        upd * before + cz * rec[:, :width] + cr * rec[:, width : 2 * width]
        + cn * rec[:, 2 * width :] + off
    )
    out[pl.ds(1, number, 2), :] = odd[pl.ds(8, number), :]

    @pl.when(me < count - 1)
    def _():
        row_copy().wait_send()

    for condition, some in map_copies + state_copies:
        @pl.when(condition)
        def _():
            for copy in some:
                copy.wait_send()


def solution(mesh):
    count = mesh.shape["seq"]

    def per_device(inputs, guesses, initial, w_input, w_hidden, biases):
        steps, width = guesses.shape
        full = width + TAIL
        line = pltpu.VMEM((steps, width), jnp.float32)
        return pl.pallas_call(
            functools.partial(kernel, count),
            out_shape=jax.ShapeDtypeStruct((steps, width), jnp.float32),
            in_specs=[pl.BlockSpec(memory_space=pl.ANY)] * 6,
            out_specs=pl.BlockSpec(memory_space=pltpu.VMEM),
            scratch_shapes=[
                pltpu.VMEM((steps, width), jnp.float32),
                pltpu.VMEM((width,), jnp.float32),
                pltpu.VMEM((width, 3 * width), jnp.float32),
                pltpu.VMEM((width, 3 * width), jnp.float32),
                pltpu.VMEM((3 * width,), jnp.float32),
                pltpu.VMEM((2 * width, 6 * width), jnp.bfloat16),
                pltpu.VMEM((steps // 2, full, width), jnp.float32),
                pltpu.VMEM((steps + 8, width), jnp.float32),
                pltpu.VMEM((8, width), jnp.float32),
                pltpu.VMEM((16, 3 * width), jnp.float32),
                pltpu.VMEM((5, steps, width), jnp.float32),
                pltpu.VMEM((steps // 2 + 8, width), jnp.float32),
                pltpu.VMEM((2, full, width), jnp.float32),
                pltpu.VMEM((2, full, width), jnp.float32),
                pltpu.VMEM((full, width), jnp.float32),
                pltpu.VMEM((8, width), jnp.float32),
                pltpu.VMEM((2, 8, width), jnp.float32),
                pltpu.SemaphoreType.DMA((6,)),
                pltpu.SemaphoreType.DMA,
                pltpu.SemaphoreType.DMA,
                pltpu.SemaphoreType.DMA((2,)),
                pltpu.SemaphoreType.DMA((2,)),
                pltpu.SemaphoreType.DMA((2, 4)),
                pltpu.SemaphoreType.DMA,
            ],
            compiler_params=pltpu.CompilerParams(
                collective_id=0, has_side_effects=True, vmem_limit_bytes=56 * 2**20),
        )(inputs, guesses, initial, w_input, w_hidden, biases)

    placed = (P(("groups", "seq"), None), P(("groups", "seq"), None), P("groups"), P(), P(), P())
    return jax.shard_map(
        per_device,
        mesh=mesh,
        in_specs=placed,
        out_specs=P(("groups", "seq"), None),
        check_vma=False,
    )
```

```python
import functools

import jax
import jax.numpy as jnp
from jax import lax
from jax.experimental import pallas as pl
from jax.experimental.pallas import tpu as pltpu
from jax.sharding import PartitionSpec as P

TAIL = 16
SENT = 8
BATCH = 16
PAIRS = 8
GROUP = 4


def split(value):
    high = value.astype(jnp.bfloat16)
    low = (value - high.astype(jnp.float32)).astype(jnp.bfloat16)
    return high, low


def product(left, right):
    lh, ll = split(left)
    rh, rl = split(right)
    parts = jnp.concatenate([rh, rl], axis=1)
    both = jnp.dot(
        jnp.concatenate([lh, ll], axis=1),
        jnp.concatenate([parts, parts], axis=0),
        preferred_element_type=jnp.float32,
    )
    width = right.shape[1]
    return both[:, :width] + both[:, width:]


def compose(early, late):
    width = late.shape[1]
    moved = product(early, late[:width])
    return moved[:width], moved[width:] + late[width:]


def column(row):
    width = row.shape[1]
    return jnp.broadcast_to(row, (width, width)).T


def gates(previous, pre, rec):
    width = previous.shape[1]
    pz, pr, pn = (pre[:, :width], pre[:, width : 2 * width], pre[:, 2 * width :])
    cz, cr, cn = (rec[:, :width], rec[:, width : 2 * width], rec[:, 2 * width :])
    update = jax.nn.sigmoid(pz + cz)
    reset = jax.nn.sigmoid(pr + cr)
    cand = jnp.tanh(pn + reset * cn)
    value = (1.0 - update) * cand + update * previous
    coef_update = (previous - cand) * update * (1.0 - update)
    coef_cand = (1.0 - update) * (1.0 - cand * cand) * reset
    coef_reset = (1.0 - update) * (1.0 - cand * cand) * cn * reset * (1.0 - reset)
    offset = value - (update * previous + coef_update * cz + coef_cand * cn + coef_reset * cr)
    return update, coef_update, coef_reset, coef_cand, offset


def store(ref, new):
    width = new[0].shape[0]
    ref[:width, :] = new[0]
    ref[width:, :] = new[1]


def kernel(
    count,
    inputs_hbm, guesses_hbm, initial_hbm, w_input_hbm, w_hidden_hbm, biases_hbm, out,
    inputs, initial, w_input, w_hidden, biases, packed,
    maps, prev, landed, pre_first, coefs, odd, arrived, incl, excl, state, state_next,
    load_sem, row_send, row_recv, map_send, map_recv, state_send, state_recv,
):
    steps, width = inputs.shape
    me = lax.axis_index("seq")
    plane, place = lax.div(me, GROUP), lax.rem(me, GROUP)
    early_plane = plane == 0
    late_plane = me >= count - GROUP
    more = jnp.logical_not(late_plane)
    later_plane = jnp.logical_not(early_plane)
    odd_place = lax.rem(me, 2) == 1
    far = place >= 2
    both = jnp.logical_and

    def row_copy():
        return pltpu.make_async_remote_copy(
            src_ref=prev.at[pl.ds(steps, 8)], dst_ref=landed,
            send_sem=row_send, recv_sem=row_recv, device_id={"seq": me + 1})

    def map_copy(src, slot, sem, device):
        return pltpu.make_async_remote_copy(
            src_ref=src.at[pl.ds(0, width + SENT)],
            dst_ref=arrived.at[slot, pl.ds(0, width + SENT)],
            send_sem=map_send.at[sem], recv_sem=map_recv.at[slot],
            device_id={"seq": device})

    def state_copy(slot, which, device):
        return pltpu.make_async_remote_copy(
            src_ref=state_next.at[slot], dst_ref=state,
            send_sem=state_send.at[slot, which], recv_sem=state_recv,
            device_id={"seq": device})

    total = maps.at[steps // 2 - 1]
    whole_pair = incl.at[0]
    column_next = plane * GROUP + GROUP + jnp.where(far, 2, 0)
    map_copies = [
        (both(jnp.logical_not(odd_place), me > 0), [map_copy(total, 0, 0, me + 1)]),
        (both(place == 1, later_plane),
         [map_copy(whole_pair, 1, 0, me + 2)]),
        (both(both(place == 3, later_plane), more), [map_copy(whole_pair, 1, 0, me - 2)]),
        (both(place == 3, later_plane), [map_copy(arrived.at[1], 1, 1, me - 1)]),
    ]
    state_copies = [
        (me == 0, [state_copy(0, 0, 1)]),
        (me == 1, [state_copy(0, 0, 3), state_copy(0, 1, 2)]),
        (both(both(odd_place, more), me >= 3),
         [state_copy(1, 0, column_next + 1), state_copy(1, 1, column_next)]),
        (both(me == 3, more), [state_copy(1, 2, GROUP), state_copy(1, 3, GROUP + 1)]),
    ]

    def start(entry):
        @pl.when(entry[0])
        def _():
            for copy in entry[1]:
                copy.start()

    loads = [
        pltpu.make_async_copy(src, dst, load_sem.at[k])
        for k, (src, dst) in enumerate([
            (guesses_hbm, prev.at[pl.ds(8, steps)]), (initial_hbm, initial),
            (w_hidden_hbm, w_hidden), (inputs_hbm, inputs),
            (w_input_hbm, w_input), (biases_hbm, biases)])
    ]
    for load in loads:
        load.start()

    barrier = pltpu.get_barrier_semaphore()

    def here(condition, device):
        @pl.when(condition)
        def _():
            pl.semaphore_signal(barrier, 1, device_id={"seq": device})

    here(me > 0, me - 1)
    here(odd_place, me - 1)
    here(far, plane * GROUP + jnp.where(both(later_plane, place == 2), 3, 1))
    here(both(both(place == 1, later_plane), more), me + 2)
    here(later_plane, plane * GROUP - jnp.where(jnp.logical_or(far, plane == 1), 1, 3))
    arrived[:, width + SENT :, :] = jnp.zeros((2, TAIL - SENT, width), jnp.float32)

    for load in loads[:3]:
        load.wait()

    prev[pl.ds(0, 8), :] = jnp.broadcast_to(initial[...][None, :], (8, width))
    high, low = split(w_hidden[...])
    for half in range(2):
        packed[half * width : (half + 1) * width, : 3 * width] = high
        packed[half * width : (half + 1) * width, 3 * width :] = low

    def recurrent(rows):
        both = jnp.dot(
            jnp.concatenate(split(rows), axis=1), packed[...],
            preferred_element_type=jnp.float32)
        return both[:, : 3 * width] + both[:, 3 * width :]

    previous = prev[pl.ds(7, steps), :]
    rec = recurrent(previous)
    for load in loads[3:]:
        load.wait()
    pre = product(inputs[...], w_input[...]) + biases[...][None, :]
    pre_first[...] = pre[:16]
    copies = (me < count - 1).astype(jnp.int32)
    for condition, some in map_copies + state_copies:
        copies += len(some) * condition.astype(jnp.int32)

    pl.semaphore_wait(barrier, copies)

    @pl.when(me < count - 1)
    def _():
        row_copy().start()

    for k, part in enumerate(gates(previous, pre, rec)):
        coefs[k] = part

    rows = lax.broadcasted_iota(jnp.int32, (width, width), 0)
    cols = lax.broadcasted_iota(jnp.int32, (width, width), 1)
    top = lax.broadcasted_iota(jnp.int32, (TAIL, width), 0) == 0

    def step_map(t):
        one = pl.ds(t, 1)
        upd, cz, cr, cn, off = [coefs[k, one, :] for k in range(5)]
        body = (
            jnp.where(rows == cols, upd, 0.0)
            + cz * w_hidden[:, :width]
            + cr * w_hidden[:, width : 2 * width]
            + cn * w_hidden[:, 2 * width :]
        )
        return jnp.concatenate([body, jnp.where(top, off, 0.0)], axis=0)

    def pairs(start, size):
        news = [compose(step_map(2 * i), step_map(2 * i + 1))
                for i in [start + k for k in range(size)]]
        for k, new in enumerate(news):
            store(maps.at[start + k], new)

    number = steps // 2
    half = (number + PAIRS) // 2
    pairs(PAIRS, half - PAIRS)

    @pl.when(me > 0)
    def _():
        row_copy().wait_recv()
        prev[pl.ds(7, 1), :] = landed[pl.ds(7, 1), :]

    fixed = prev[pl.ds(7, 16), :]
    parts = gates(fixed, pre_first[...], recurrent(fixed))
    pairs(half, number - half)
    for k, part in enumerate(parts):
        coefs[k, :16, :] = part
    pairs(0, PAIRS)

    def sweep(first, stride, distance, number):
        batch = min(BATCH, number)

        def some(start, size):
            where = [start + stride * j for j in range(size)]
            news = [compose(maps[i - distance], maps[i]) for i in where]
            for i, new in zip(where, news):
                store(maps.at[i], new)

        def body(j, _):
            some(first + j * (stride * batch), batch)
            return 0

        whole = number // batch
        if whole > 1:
            lax.fori_loop(0, whole, body, 0)
        else:
            some(first, batch)
        if number % batch:
            some(first + whole * batch * stride, number % batch)

    distance = 1
    while distance < number:
        sweep(2 * distance - 1, 2 * distance, distance, number // (2 * distance))
        distance *= 2

    down = []
    distance = number // 4
    while distance >= 1:
        down.append((3 * distance - 1, 2 * distance, distance, number // (2 * distance) - 1))
        distance //= 2

    def applied(row, ref):
        moved = jnp.sum(column(row) * ref[:width, :], axis=0, keepdims=True)
        return moved + ref[width : width + 1, :]

    def arrival(slot):
        map_copy(total, slot, 0, me + 1).wait_recv()

    def wait_state():
        state_copy(0, 0, me + 1).wait_recv()

    @pl.when(me == 0)
    def _():
        state[...] = jnp.broadcast_to(initial[...][None, :], state.shape)
        state_next[0] = jnp.broadcast_to(applied(state[0:1, :], total), (8, width))

    start(state_copies[0])
    start(map_copies[0])
    excl[:width, :] = jnp.where(rows == cols, 1.0, 0.0)
    excl[width:, :] = jnp.zeros((TAIL, width), jnp.float32)
    for item in down[:-2]:
        sweep(*item)

    @pl.when(me == 1)
    def _():
        wait_state()
        state_next[0] = jnp.broadcast_to(applied(state[0:1, :], total), (8, width))

    start(state_copies[1])

    @pl.when(both(odd_place, me >= 3))
    def _():
        arrival(0)
        store(incl.at[0], compose(arrived[0], total[...]))
        excl[...] = arrived[0]

    for entry in map_copies[1:3]:
        start(entry)
    for item in down[-2:-1]:
        sweep(*item)

    @pl.when(me == 3)
    def _():
        wait_state()
        state_next[1] = jnp.broadcast_to(applied(state[0:1, :], whole_pair), (8, width))

    @pl.when(both(later_plane, jnp.logical_or(far, both(place == 1, more))))
    def _():
        arrival(1)

    start(map_copies[3])
    second = both(both(plane == 1, more), place == 3)

    @pl.when(both(both(later_plane, more), place == 1))
    def _():
        store(incl.at[1], compose(incl[0], arrived[1]))

    @pl.when(both(both(plane > 1, more), place == 3))
    def _():
        store(incl.at[1], compose(arrived[1], incl[0]))

    @pl.when(second)
    def _():
        wait_state()
        row = applied(applied(state[0:1, :], arrived.at[1]), whole_pair)
        state_next[1] = jnp.broadcast_to(row, (8, width))

    @pl.when(both(both(both(later_plane, more), odd_place), jnp.logical_not(second)))
    def _():
        wait_state()
        state_next[1] = jnp.broadcast_to(applied(state[0:1, :], incl.at[1]), (8, width))

    start(state_copies[2])
    start(state_copies[3])

    @pl.when(both(later_plane, place == 2))
    def _():
        excl[...] = arrived[1]

    @pl.when(both(later_plane, place == 3))
    def _():
        store(excl, compose(arrived[1], arrived[0]))

    for item in down[-1:]:
        sweep(*item)

    @pl.when(jnp.logical_or(
        me == 2, both(later_plane, jnp.logical_or(late_plane, jnp.logical_not(odd_place)))))
    def _():
        wait_state()

    entry = applied(state[0:1, :], excl)
    across = column(entry)
    odd[0:8, :] = jnp.broadcast_to(entry, (8, width))

    for j in range(0, number, 8):
        lines = []
        for i in range(j, j + 8):
            line = jnp.sum(across * maps[i, :width, :], axis=0, keepdims=True)
            lines.append(line + maps[i, width : width + 1, :])
        odd[j + 8 : j + 16, :] = jnp.concatenate(lines, axis=0)

    before = odd[pl.ds(7, number), :]
    rec = recurrent(before)
    even = pl.ds(0, number, 2)
    upd, cz, cr, cn, off = [coefs[k, even, :] for k in range(5)]
    out[even, :] = (
        upd * before + cz * rec[:, :width] + cr * rec[:, width : 2 * width]
        + cn * rec[:, 2 * width :] + off
    )
    out[pl.ds(1, number, 2), :] = odd[pl.ds(8, number), :]

    @pl.when(me < count - 1)
    def _():
        row_copy().wait_send()

    for condition, some in map_copies + state_copies:
        @pl.when(condition)
        def _():
            for copy in some:
                copy.wait_send()


def moved_out(src, dst, sem):
    copy = pltpu.make_async_copy(src, dst, sem)
    copy.start()
    copy.wait()


def solution(mesh):
    count = mesh.shape["seq"]

    def per_device(inputs, guesses, initial, w_input, w_hidden, biases):
        steps, width = guesses.shape
        full = width + TAIL
        line = pltpu.VMEM((steps, width), jnp.float32)
        rows = pl.pallas_call(
            functools.partial(kernel, count),
            out_shape=jax.ShapeDtypeStruct((steps, width), jnp.float32),
            in_specs=[pl.BlockSpec(memory_space=pl.ANY)] * 6,
            out_specs=pl.BlockSpec(memory_space=pltpu.VMEM),
            scratch_shapes=[
                pltpu.VMEM((steps, width), jnp.float32),
                pltpu.VMEM((width,), jnp.float32),
                pltpu.VMEM((width, 3 * width), jnp.float32),
                pltpu.VMEM((width, 3 * width), jnp.float32),
                pltpu.VMEM((3 * width,), jnp.float32),
                pltpu.VMEM((2 * width, 6 * width), jnp.bfloat16),
                pltpu.VMEM((steps // 2, full, width), jnp.float32),
                pltpu.VMEM((steps + 8, width), jnp.float32),
                pltpu.VMEM((8, width), jnp.float32),
                pltpu.VMEM((16, 3 * width), jnp.float32),
                pltpu.VMEM((5, steps, width), jnp.float32),
                pltpu.VMEM((steps // 2 + 8, width), jnp.float32),
                pltpu.VMEM((2, full, width), jnp.float32),
                pltpu.VMEM((2, full, width), jnp.float32),
                pltpu.VMEM((full, width), jnp.float32),
                pltpu.VMEM((8, width), jnp.float32),
                pltpu.VMEM((2, 8, width), jnp.float32),
                pltpu.SemaphoreType.DMA((6,)),
                pltpu.SemaphoreType.DMA,
                pltpu.SemaphoreType.DMA,
                pltpu.SemaphoreType.DMA((2,)),
                pltpu.SemaphoreType.DMA((2,)),
                pltpu.SemaphoreType.DMA((2, 4)),
                pltpu.SemaphoreType.DMA,
            ],
            compiler_params=pltpu.CompilerParams(
                collective_id=0, has_side_effects=True, vmem_limit_bytes=56 * 2**20),
        )(inputs, guesses, initial, w_input, w_hidden, biases)
        return pl.pallas_call(
            moved_out,
            out_shape=jax.ShapeDtypeStruct((steps, width), jnp.float32),
            in_specs=[pl.BlockSpec(memory_space=pl.ANY)],
            out_specs=pl.BlockSpec(memory_space=pl.ANY),
            scratch_shapes=[pltpu.SemaphoreType.DMA],
            compiler_params=pltpu.CompilerParams(vmem_limit_bytes=56 * 2**20),
        )(rows)

    placed = (P(("groups", "seq"), None), P(("groups", "seq"), None), P("groups"), P(), P(), P())
    return jax.shard_map(
        per_device,
        mesh=mesh,
        in_specs=placed,
        out_specs=P(("groups", "seq"), None),
        check_vma=False,
    )
```

```python
import functools

import jax
import jax.numpy as jnp
from jax import lax
from jax.experimental import pallas as pl
from jax.experimental.pallas import tpu as pltpu
from jax.sharding import PartitionSpec as P

TAIL = 16
SENT = 8
BATCH = 16
PAIRS = 8
GROUP = 4


def split(value):
    high = value.astype(jnp.bfloat16)
    low = (value - high.astype(jnp.float32)).astype(jnp.bfloat16)
    return high, low


def product(left, right):
    lh, ll = split(left)
    rh, rl = split(right)
    parts = jnp.concatenate([rh, rl], axis=1)
    both = jnp.dot(
        jnp.concatenate([lh, ll], axis=1),
        jnp.concatenate([parts, parts], axis=0),
        preferred_element_type=jnp.float32,
    )
    width = right.shape[1]
    return both[:, :width] + both[:, width:]


def compose(early, late):
    width = late.shape[1]
    moved = product(early, late[:width])
    return moved[:width], moved[width:] + late[width:]


def column(row):
    width = row.shape[1]
    return jnp.broadcast_to(row, (width, width)).T


def gates(previous, pre, rec):
    width = previous.shape[1]
    pz, pr, pn = (pre[:, :width], pre[:, width : 2 * width], pre[:, 2 * width :])
    cz, cr, cn = (rec[:, :width], rec[:, width : 2 * width], rec[:, 2 * width :])
    update = jax.nn.sigmoid(pz + cz)
    reset = jax.nn.sigmoid(pr + cr)
    cand = jnp.tanh(pn + reset * cn)
    value = (1.0 - update) * cand + update * previous
    coef_update = (previous - cand) * update * (1.0 - update)
    coef_cand = (1.0 - update) * (1.0 - cand * cand) * reset
    coef_reset = (1.0 - update) * (1.0 - cand * cand) * cn * reset * (1.0 - reset)
    offset = value - (update * previous + coef_update * cz + coef_cand * cn + coef_reset * cr)
    return update, coef_update, coef_reset, coef_cand, offset


def store(ref, new):
    width = new[0].shape[0]
    ref[:width, :] = new[0]
    ref[width:, :] = new[1]


def kernel(
    count,
    inputs_hbm, guesses_hbm, initial_hbm, w_input_hbm, w_hidden_hbm, biases_hbm, out,
    inputs, initial, w_input, w_hidden, biases, packed,
    maps, prev, landed, pre_first, coefs, odd, arrived, incl, excl, state, state_next,
    load_sem, row_send, row_recv, map_send, map_recv, state_send, state_recv,
):
    steps, width = inputs.shape
    me = lax.axis_index("seq")
    plane, place = lax.div(me, GROUP), lax.rem(me, GROUP)
    early_plane = plane == 0
    late_plane = me >= count - GROUP
    more = jnp.logical_not(late_plane)
    later_plane = jnp.logical_not(early_plane)
    odd_place = lax.rem(me, 2) == 1
    far = place >= 2
    both = jnp.logical_and

    def row_copy():
        return pltpu.make_async_remote_copy(
            src_ref=prev.at[pl.ds(steps, 8)], dst_ref=landed,
            send_sem=row_send, recv_sem=row_recv, device_id={"seq": me + 1})

    def map_copy(src, slot, sem, device):
        return pltpu.make_async_remote_copy(
            src_ref=src.at[pl.ds(0, width + SENT)],
            dst_ref=arrived.at[slot, pl.ds(0, width + SENT)],
            send_sem=map_send.at[sem], recv_sem=map_recv.at[slot],
            device_id={"seq": device})

    def state_copy(slot, which, device):
        return pltpu.make_async_remote_copy(
            src_ref=state_next.at[slot], dst_ref=state,
            send_sem=state_send.at[slot, which], recv_sem=state_recv,
            device_id={"seq": device})

    total = maps.at[steps // 2 - 1]
    whole_pair = incl.at[0]
    column_next = plane * GROUP + GROUP + jnp.where(far, 2, 0)
    map_copies = [
        (both(jnp.logical_not(odd_place), me > 0), [map_copy(total, 0, 0, me + 1)]),
        (both(place == 1, later_plane),
         [map_copy(whole_pair, 1, 0, me + 2)]),
        (both(both(place == 3, later_plane), more), [map_copy(whole_pair, 1, 0, me - 2)]),
        (both(place == 3, later_plane), [map_copy(arrived.at[1], 1, 1, me - 1)]),
    ]
    state_copies = [
        (me == 0, [state_copy(0, 0, 1)]),
        (me == 1, [state_copy(0, 0, 3), state_copy(0, 1, 2)]),
        (both(both(odd_place, more), me >= 3),
         [state_copy(1, 0, column_next + 1), state_copy(1, 1, column_next)]),
        (both(me == 3, more), [state_copy(1, 2, GROUP), state_copy(1, 3, GROUP + 1)]),
    ]

    def start(entry):
        @pl.when(entry[0])
        def _():
            for copy in entry[1]:
                copy.start()

    loads = [
        pltpu.make_async_copy(src, dst, load_sem.at[k])
        for k, (src, dst) in enumerate([
            (guesses_hbm, prev.at[pl.ds(8, steps)]), (initial_hbm, initial),
            (w_hidden_hbm, w_hidden), (inputs_hbm, inputs),
            (w_input_hbm, w_input), (biases_hbm, biases)])
    ]
    for load in loads:
        load.start()

    barrier = pltpu.get_barrier_semaphore()

    def here(condition, device):
        @pl.when(condition)
        def _():
            pl.semaphore_signal(barrier, 1, device_id={"seq": device})

    here(me > 0, me - 1)
    here(odd_place, me - 1)
    here(far, plane * GROUP + jnp.where(both(later_plane, place == 2), 3, 1))
    here(both(both(place == 1, later_plane), more), me + 2)
    here(later_plane, plane * GROUP - jnp.where(jnp.logical_or(far, plane == 1), 1, 3))
    arrived[:, width + SENT :, :] = jnp.zeros((2, TAIL - SENT, width), jnp.float32)

    for load in loads[:3]:
        load.wait()

    prev[pl.ds(0, 8), :] = jnp.broadcast_to(initial[...][None, :], (8, width))
    high, low = split(w_hidden[...])
    for half in range(2):
        packed[half * width : (half + 1) * width, : 3 * width] = high
        packed[half * width : (half + 1) * width, 3 * width :] = low

    def recurrent(rows):
        both = jnp.dot(
            jnp.concatenate(split(rows), axis=1), packed[...],
            preferred_element_type=jnp.float32)
        return both[:, : 3 * width] + both[:, 3 * width :]

    previous = prev[pl.ds(7, steps), :]
    rec = recurrent(previous)
    for load in loads[3:]:
        load.wait()
    pre = product(inputs[...], w_input[...]) + biases[...][None, :]
    pre_first[...] = pre[:16]
    for k, part in enumerate(gates(previous, pre, rec)):
        coefs[k] = part

    copies = (me < count - 1).astype(jnp.int32)
    for condition, some in map_copies + state_copies:
        copies += len(some) * condition.astype(jnp.int32)

    pl.semaphore_wait(barrier, copies)

    @pl.when(me < count - 1)
    def _():
        row_copy().start()

    rows = lax.broadcasted_iota(jnp.int32, (width, width), 0)
    cols = lax.broadcasted_iota(jnp.int32, (width, width), 1)
    top = lax.broadcasted_iota(jnp.int32, (TAIL, width), 0) == 0

    def step_map(t):
        one = pl.ds(t, 1)
        upd, cz, cr, cn, off = [coefs[k, one, :] for k in range(5)]
        body = (
            jnp.where(rows == cols, upd, 0.0)
            + cz * w_hidden[:, :width]
            + cr * w_hidden[:, width : 2 * width]
            + cn * w_hidden[:, 2 * width :]
        )
        return jnp.concatenate([body, jnp.where(top, off, 0.0)], axis=0)

    def pairs(start, size):
        news = [compose(step_map(2 * i), step_map(2 * i + 1))
                for i in [start + k for k in range(size)]]
        for k, new in enumerate(news):
            store(maps.at[start + k], new)

    number = steps // 2
    for k in range(2):
        pairs(PAIRS + k * (number - PAIRS) // 2, (number - PAIRS) // 2)

    @pl.when(me > 0)
    def _():
        row_copy().wait_recv()
        prev[pl.ds(7, 1), :] = landed[pl.ds(7, 1), :]
        fixed = prev[pl.ds(7, 16), :]
        for k, part in enumerate(gates(fixed, pre_first[...], recurrent(fixed))):
            coefs[k, :16, :] = part

    pairs(0, PAIRS)

    def sweep(first, stride, distance, number):
        batch = min(BATCH, number)

        def some(start, size):
            where = [start + stride * j for j in range(size)]
            news = [compose(maps[i - distance], maps[i]) for i in where]
            for i, new in zip(where, news):
                store(maps.at[i], new)

        def body(j, _):
            some(first + j * (stride * batch), batch)
            return 0

        whole = number // batch
        if whole > 1:
            lax.fori_loop(0, whole, body, 0)
        else:
            some(first, batch)
        if number % batch:
            some(first + whole * batch * stride, number % batch)

    distance = 1
    while distance < number:
        sweep(2 * distance - 1, 2 * distance, distance, number // (2 * distance))
        distance *= 2

    down = []
    distance = number // 4
    while distance >= 1:
        down.append((3 * distance - 1, 2 * distance, distance, number // (2 * distance) - 1))
        distance //= 2

    def applied(row, ref):
        moved = jnp.sum(column(row) * ref[:width, :], axis=0, keepdims=True)
        return moved + ref[width : width + 1, :]

    def arrival(slot):
        map_copy(total, slot, 0, me + 1).wait_recv()

    def wait_state():
        state_copy(0, 0, me + 1).wait_recv()

    @pl.when(me == 0)
    def _():
        state[...] = jnp.broadcast_to(initial[...][None, :], state.shape)
        state_next[0] = jnp.broadcast_to(applied(state[0:1, :], total), (8, width))

    start(state_copies[0])
    start(map_copies[0])
    excl[:width, :] = jnp.where(rows == cols, 1.0, 0.0)
    excl[width:, :] = jnp.zeros((TAIL, width), jnp.float32)
    for item in down[:-2]:
        sweep(*item)

    @pl.when(me == 1)
    def _():
        wait_state()
        state_next[0] = jnp.broadcast_to(applied(state[0:1, :], total), (8, width))

    start(state_copies[1])

    @pl.when(both(odd_place, me >= 3))
    def _():
        arrival(0)
        store(incl.at[0], compose(arrived[0], total[...]))
        excl[...] = arrived[0]

    for entry in map_copies[1:3]:
        start(entry)
    for item in down[-2:-1]:
        sweep(*item)

    @pl.when(me == 3)
    def _():
        wait_state()
        state_next[1] = jnp.broadcast_to(applied(state[0:1, :], whole_pair), (8, width))

    @pl.when(both(later_plane, jnp.logical_or(far, both(place == 1, more))))
    def _():
        arrival(1)

    start(map_copies[3])
    second = both(both(plane == 1, more), odd_place)

    @pl.when(both(both(plane > 1, more), place == 1))
    def _():
        store(incl.at[1], compose(incl[0], arrived[1]))

    @pl.when(both(both(plane > 1, more), place == 3))
    def _():
        store(incl.at[1], compose(arrived[1], incl[0]))

    @pl.when(both(second, place == 1))
    def _():
        wait_state()
        row = applied(applied(state[0:1, :], whole_pair), arrived.at[1])
        state_next[1] = jnp.broadcast_to(row, (8, width))

    @pl.when(both(second, place == 3))
    def _():
        wait_state()
        row = applied(applied(state[0:1, :], arrived.at[1]), whole_pair)
        state_next[1] = jnp.broadcast_to(row, (8, width))

    @pl.when(both(both(both(later_plane, more), odd_place), jnp.logical_not(second)))
    def _():
        wait_state()
        state_next[1] = jnp.broadcast_to(applied(state[0:1, :], incl.at[1]), (8, width))

    start(state_copies[3])
    start(state_copies[2])

    @pl.when(both(later_plane, place == 2))
    def _():
        excl[...] = arrived[1]

    @pl.when(both(later_plane, place == 3))
    def _():
        store(excl, compose(arrived[1], arrived[0]))

    for item in down[-1:]:
        sweep(*item)

    @pl.when(jnp.logical_or(
        me == 2, both(later_plane, jnp.logical_or(late_plane, jnp.logical_not(odd_place)))))
    def _():
        wait_state()

    entry = applied(state[0:1, :], excl)
    across = column(entry)
    odd[0:8, :] = jnp.broadcast_to(entry, (8, width))

    for j in range(0, number, 8):
        lines = []
        for i in range(j, j + 8):
            line = jnp.sum(across * maps[i, :width, :], axis=0, keepdims=True)
            lines.append(line + maps[i, width : width + 1, :])
        odd[j + 8 : j + 16, :] = jnp.concatenate(lines, axis=0)

    before = odd[pl.ds(7, number), :]
    rec = recurrent(before)
    even = pl.ds(0, number, 2)
    upd, cz, cr, cn, off = [coefs[k, even, :] for k in range(5)]
    out[even, :] = (
        upd * before + cz * rec[:, :width] + cr * rec[:, width : 2 * width]
        + cn * rec[:, 2 * width :] + off
    )
    out[pl.ds(1, number, 2), :] = odd[pl.ds(8, number), :]

    @pl.when(me < count - 1)
    def _():
        row_copy().wait_send()

    for condition, some in map_copies + state_copies:
        @pl.when(condition)
        def _():
            for copy in some:
                copy.wait_send()


def solution(mesh):
    count = mesh.shape["seq"]

    def per_device(inputs, guesses, initial, w_input, w_hidden, biases):
        steps, width = guesses.shape
        full = width + TAIL
        line = pltpu.VMEM((steps, width), jnp.float32)
        return pl.pallas_call(
            functools.partial(kernel, count),
            out_shape=jax.ShapeDtypeStruct((steps, width), jnp.float32),
            in_specs=[pl.BlockSpec(memory_space=pl.ANY)] * 6,
            out_specs=pl.BlockSpec(memory_space=pltpu.VMEM),
            scratch_shapes=[
                pltpu.VMEM((steps, width), jnp.float32),
                pltpu.VMEM((width,), jnp.float32),
                pltpu.VMEM((width, 3 * width), jnp.float32),
                pltpu.VMEM((width, 3 * width), jnp.float32),
                pltpu.VMEM((3 * width,), jnp.float32),
                pltpu.VMEM((2 * width, 6 * width), jnp.bfloat16),
                pltpu.VMEM((steps // 2, full, width), jnp.float32),
                pltpu.VMEM((steps + 8, width), jnp.float32),
                pltpu.VMEM((8, width), jnp.float32),
                pltpu.VMEM((16, 3 * width), jnp.float32),
                pltpu.VMEM((5, steps, width), jnp.float32),
                pltpu.VMEM((steps // 2 + 8, width), jnp.float32),
                pltpu.VMEM((2, full, width), jnp.float32),
                pltpu.VMEM((2, full, width), jnp.float32),
                pltpu.VMEM((full, width), jnp.float32),
                pltpu.VMEM((8, width), jnp.float32),
                pltpu.VMEM((2, 8, width), jnp.float32),
                pltpu.SemaphoreType.DMA((6,)),
                pltpu.SemaphoreType.DMA,
                pltpu.SemaphoreType.DMA,
                pltpu.SemaphoreType.DMA((2,)),
                pltpu.SemaphoreType.DMA((2,)),
                pltpu.SemaphoreType.DMA((2, 4)),
                pltpu.SemaphoreType.DMA,
            ],
            compiler_params=pltpu.CompilerParams(
                collective_id=0, has_side_effects=True, vmem_limit_bytes=56 * 2**20),
        )(inputs, guesses, initial, w_input, w_hidden, biases)

    placed = (P(("groups", "seq"), None), P(("groups", "seq"), None), P("groups"), P(), P(), P())
    return jax.shard_map(
        per_device,
        mesh=mesh,
        in_specs=placed,
        out_specs=P(("groups", "seq"), None),
        check_vma=False,
    )
```
